512 devices in a mesh: pipe: 64 (over y, z_lo, core), expert: 8 (over x, z_hi).
Axes of the slice: x: 4, y: 8, z: 8 (z_hi: 2, z_lo: 4; z = z_hi * 4 + z_lo), core: 2. Of those that a mesh axis runs over, the one named last changes fastest.
Arguments:
- forward_input: bfloat16 [64, 128, 4096], P('pipe', 'expert'), may hold values from -6 to 6
- forward_route: int32 [64, 128, 2], P('pipe', 'expert'), may hold values from 0 to 7, as said below
- forward_gates: float32 [64, 128, 2], P('pipe', 'expert'), may hold values from 0.2 to 2
- backward_cotangent: bfloat16 [64, 128, 4096], P('pipe', 'expert'), may hold values from -6 to 6
- backward_route: int32 [64, 128, 2], P('pipe', 'expert'), may hold values from 0 to 7, as said below
- backward_gates: float32 [64, 128, 2], P('pipe', 'expert'), may hold values from 0.2 to 2
- gate_up_weight: bfloat16 [64, 8, 2048, 512], P('pipe', 'expert'), may hold values from -0.09375 to 0.09375
- down_weight: bfloat16 [64, 8, 1024, 512], P('pipe', 'expert'), may hold values from -0.1875 to 0.1875
- saved_projections: bfloat16 [64, 8, 576, 256], P('pipe', 'expert'), may hold values from -4 to 4
Outputs:
- next_input: bfloat16 [64, 128, 4096], P('pipe', 'expert')
- prior_gradient: bfloat16 [64, 128, 4096], P('pipe', 'expert')
The draws below stay inside these ranges and needn't reach their ends.
Inputs may be any that keep to these rules, and one draw needn't show every extreme that they name: `forward_route`: each token names 2 different experts. In every section one expert, drawn afresh for each section, is named by exactly 9 tokens of every source; each other expert by at most 4 tokens of one source, the remaining choices of a source being spread over the other experts as evenly as possible. `backward_route`: as for forward_route, with its own busiest experts.
All inputs are finite; a program needn't handle non-finite values.
Results may differ from the reference program's by a relative error of at most 0.0058.
Values may be sent and summed in bfloat16 or wider, within the bound.
A program may use at most 64 MiB of HBM per device.

```python
import math
import jax
import jax.numpy as jnp
from jax import lax

D = 4096
HID = 1024
GROUP = 8
TOK = 16
SECTIONS = 8
EXPERTS = 8
TOPK = 2
CAP = 9
N_PIPE = 64


def route_law(key):
    hot_key, order_key, offset_key, rotation_key, label_key = jax.random.split(key, 5)
    busiest = jnp.repeat(jax.random.randint(hot_key, (SECTIONS,), 0, EXPERTS), GROUP)

    def section_labels(one_key):
        return jax.random.permutation(one_key, EXPERTS - 1)
    others = jax.vmap(section_labels)(jax.random.split(label_key, N_PIPE))
    others = others + (others >= busiest[:, None]).astype(jnp.int32)

    def device_order(one_key):
        return jax.random.permutation(one_key, TOK)
    rank_of = jax.vmap(device_order)(jax.random.split(order_key, N_PIPE * EXPERTS)).reshape(N_PIPE, EXPERTS, TOK)
    offset = jax.random.randint(offset_key, (N_PIPE, EXPERTS, 1), 0, EXPERTS - 1)
    rotation = jax.random.randint(rotation_key, (N_PIPE, EXPERTS, TOK, 1), 0, TOPK)
    is_busy = rank_of < CAP
    first_pick = jnp.where(is_busy, rank_of * (TOPK - 1), CAP * (TOPK - 1) + (rank_of - CAP) * TOPK) + offset
    picked = []
    for column in range(TOPK):
        slot_pick = jnp.where(is_busy, column - 1, column)
        pick_index = (first_pick + slot_pick) % (EXPERTS - 1)
        other_expert = jnp.take_along_axis(others, pick_index.reshape(N_PIPE, EXPERTS * TOK), axis=1).reshape(N_PIPE, EXPERTS, TOK)
        chosen = jnp.where(jnp.logical_and(is_busy, column == 0), busiest[:, None, None], other_expert)
        picked.append(chosen)
    stacked = jnp.stack(picked, axis=-1)
    turned = (lax.broadcasted_iota(jnp.int32, (1, 1, 1, TOPK), 3) + rotation) % TOPK
    stacked = jnp.take_along_axis(stacked, turned, axis=3)
    return stacked.reshape(N_PIPE, EXPERTS * TOK, TOPK).astype(jnp.int32)


def draw_forward_route(key, part):
    key = jax.random.fold_in(key, 11)
    return route_law(key)


def draw_backward_route(key, part):
    key = jax.random.fold_in(key, 12)
    return route_law(key)


def steps_of(stream_key, dims, cuts, least, top_value):
    gain = 1.0
    for axis_at, parts in cuts:
        steps = jax.random.uniform(jax.random.fold_in(jax.random.fold_in(stream_key, 6), axis_at), (parts,), jnp.float32, least / len(cuts), top_value / len(cuts))
        gain = gain * jnp.repeat(jnp.exp(steps), dims[axis_at] // parts).reshape((-1,) + (1,) * (len(dims) - 1 - axis_at))
    return gain


def scatter_about(key, shape, scale, bound, cuts=(), held_as=jnp.bfloat16):
    array = scale * jax.random.normal(key, shape, jnp.float32)
    if cuts:
        array = array * steps_of(key, shape, cuts, -0.22, 0.18)
    return jnp.clip(array, -bound, bound).astype(held_as)


def setup_inputs(seed: int = 0) -> dict:
    key_list = jax.random.split(jax.random.key(seed), 10)
    forward_input = scatter_about(key_list[0], (N_PIPE, EXPERTS * TOK, D), 1.0, 6.0, ((0, 64), (1, 8)))
    forward_route = draw_forward_route(jax.random.fold_in(key_list[9], 71), 0)
    forward_gates = jnp.clip(jnp.exp(math.log(2.0) - 2.3025851 * jax.random.uniform(key_list[2], (N_PIPE, EXPERTS * TOK, TOPK), jnp.float32) ** steps_of(key_list[2], (N_PIPE, EXPERTS * TOK, TOPK), ((0, 64), (1, 8)), -0.2, 0.2)), 0.2, 2.0)
    backward_cotangent = scatter_about(key_list[3], (N_PIPE, EXPERTS * TOK, D), 1.0, 6.0, ((0, 64), (1, 8)))
    backward_route = draw_backward_route(jax.random.fold_in(key_list[9], 71), 0)
    backward_gates = jnp.clip(jnp.exp(math.log(2.0) - 2.3025851 * jax.random.uniform(key_list[5], (N_PIPE, EXPERTS * TOK, TOPK), jnp.float32) ** steps_of(key_list[5], (N_PIPE, EXPERTS * TOK, TOPK), ((0, 64), (1, 8)), -0.2, 0.2)), 0.2, 2.0)
    gate_up_weight = scatter_about(key_list[6], (N_PIPE, EXPERTS, 2 * HID, D // GROUP), D ** -0.5, 0.09375, ((0, 64), (1, 8)))
    down_weight = scatter_about(key_list[7], (N_PIPE, EXPERTS, HID, D // GROUP), HID ** -0.5, 0.1875, ((0, 64), (1, 8)))
    saved_projections = scatter_about(key_list[8], (N_PIPE, EXPERTS, GROUP * EXPERTS * CAP, 2 * HID // GROUP), 1.0, 4.0, ((0, 64), (1, 8)))
    return {"forward_input": forward_input, "forward_route": forward_route, "forward_gates": forward_gates, "backward_cotangent": backward_cotangent, "backward_route": backward_route, "backward_gates": backward_gates, "gate_up_weight": gate_up_weight, "down_weight": down_weight, "saved_projections": saved_projections}


def silu_terms(gate_pre):
    logistic = jax.nn.sigmoid(gate_pre)
    return gate_pre * logistic, logistic * (1.0 + gate_pre * (1.0 - logistic))


def expert_forward(input_row_block, gate_up_product, down_projected_rows):
    hidden_units = down_projected_rows.shape[1]
    projected_rows = jnp.einsum("ahl,atl->aht", input_row_block.astype(jnp.float32), gate_up_product.astype(jnp.float32))
    activated, unused_slope = silu_terms(projected_rows[..., :hidden_units])
    hidden_activation = (activated * projected_rows[..., hidden_units:]).astype(jnp.bfloat16)
    produced_rows = jnp.einsum("yet,ytx->yex", hidden_activation.astype(jnp.float32), down_projected_rows.astype(jnp.float32))
    return produced_rows.astype(jnp.bfloat16)


def expert_backward(gradient_block_rows, stashed, gate_up_product, down_projected_rows):
    hidden_units = down_projected_rows.shape[1]
    hidden_gradient = jnp.einsum("ahl,atl->aht", gradient_block_rows.astype(jnp.float32), down_projected_rows.astype(jnp.float32))
    gate_pre = stashed[..., :hidden_units].astype(jnp.float32)
    up_pre = stashed[..., hidden_units:].astype(jnp.float32)
    activated, slope = silu_terms(gate_pre)
    preactivation_gradient = jnp.concatenate([hidden_gradient * up_pre * slope, hidden_gradient * activated], axis=-1).astype(jnp.bfloat16)
    produced_rows = jnp.einsum("yet,ytx->yex", preactivation_gradient.astype(jnp.float32), gate_up_product.astype(jnp.float32))
    return produced_rows.astype(jnp.bfloat16)


def rank_slots(route, experts):
    labels = lax.broadcasted_iota(jnp.int32, (1, 1, experts), 2)
    hits = (route[:, :, None] == labels).astype(jnp.int32)
    row_hits = jnp.sum(hits, axis=1)
    before = jnp.cumsum(row_hits, axis=0) - row_hits
    return jnp.sum(hits * before[:, None, :], axis=2)


def source_ranks(source_route):
    return rank_slots(source_route, EXPERTS)


def section_routes(route_all):
    sources = GROUP * EXPERTS
    per_source = route_all.reshape(sources, TOK, TOPK)
    slot_rank = jax.vmap(source_ranks)(per_source)
    source_ids = lax.broadcasted_iota(jnp.int32, (sources, TOK, TOPK), 0)
    row_ids = source_ids * TOK + lax.broadcasted_iota(jnp.int32, (sources, TOK, TOPK), 1)
    target = per_source * (sources * CAP) + source_ids * CAP + slot_rank
    source_rows = jnp.full((EXPERTS * sources * CAP,), sources * TOK, jnp.int32)
    source_rows = source_rows.at[target.reshape(-1)].set(row_ids.reshape(-1))
    return source_rows.reshape(EXPERTS, sources * CAP), target.reshape(sources * TOK, TOPK)


def combine_rows(flat_out, position, gates):
    gathered = jnp.take(flat_out, position, axis=0).astype(jnp.float32)
    return jnp.sum(gathered * gates[:, :, None], axis=1).astype(jnp.bfloat16)


def join_columns(slab):
    experts_here = slab.shape[1]
    rows_here = slab.shape[2]
    return jnp.transpose(slab, (1, 2, 0, 3)).reshape(experts_here, rows_here, -1)


def section_work(operands):
    forward_input, forward_route, forward_gates, backward_cotangent, backward_route, backward_gates, gate_up_slab, down_slab, saved_slab = operands
    model_width = forward_input.shape[1]
    gate_up_product = join_columns(gate_up_slab)
    down_projected_rows = join_columns(down_slab)
    units = saved_slab.shape[3] // 2
    slot_rows = saved_slab.shape[2]
    stashed = saved_slab.reshape(GROUP, EXPERTS, slot_rows, 2, units)
    stashed = jnp.transpose(stashed, (1, 2, 3, 0, 4)).reshape(EXPERTS, slot_rows, 2 * GROUP * units)
    source_rows, flat_index = section_routes(forward_route)
    input_row_block = jnp.take(forward_input, source_rows, axis=0, mode="fill", fill_value=0)
    produced_rows = expert_forward(input_row_block, gate_up_product, down_projected_rows).reshape(-1, model_width)
    section_output = combine_rows(produced_rows, flat_index, forward_gates)
    source_rows, flat_index = section_routes(backward_route)
    gradient_block_rows = jnp.take(backward_cotangent, source_rows, axis=0, mode="fill", fill_value=0)
    returned = expert_backward(gradient_block_rows, stashed, gate_up_product, down_projected_rows).reshape(-1, model_width)
    section_gradient = combine_rows(returned, flat_index, backward_gates)
    return section_output, section_gradient


def reference(forward_input, forward_route, forward_gates, backward_cotangent, backward_route, backward_gates, gate_up_weight, down_weight, saved_projections):
    def per_section(values):
        return values.reshape((SECTIONS, GROUP * values.shape[1]) + values.shape[2:])

    def slabs(values):
        return values.reshape((SECTIONS, GROUP) + values.shape[1:])

    outputs, gradients = lax.map(section_work, (per_section(forward_input), per_section(forward_route), per_section(forward_gates), per_section(backward_cotangent), per_section(backward_route), per_section(backward_gates), slabs(gate_up_weight), slabs(down_weight), slabs(saved_projections)))
    outputs = outputs.reshape(forward_input.shape)
    gradients = gradients.reshape(forward_input.shape)
    return jnp.roll(outputs, GROUP, axis=0), jnp.roll(gradients, -GROUP, axis=0)
```

```python
import functools

import jax
import jax.numpy as jnp
import numpy as np
from jax import lax
from jax.experimental import pallas as pl
from jax.experimental.pallas import tpu as pltpu
from jax.sharding import PartitionSpec as P

GROUP = 8
BASE = 4
OVER = 5
ZN = 16
XN = 4
LINE = 4
CHUNK = ZN * (BASE + OVER)
MESH = pl.DeviceIdType.MESH


def permutations():
    norm_out = np.zeros((256, 256), np.float32)
    over_out = np.zeros((2, 80, 256), np.float32)
    norm_back = np.zeros((256, XN * CHUNK), np.float32)
    over_back = np.zeros((2, 256, XN * CHUNK), np.float32)
    stash = np.zeros((XN * CHUNK, XN * CHUNK), np.float32)
    for g in range(ZN):
        for x in range(XN):
            for s in range(BASE):
                norm_out[x * 64 + g * 4 + s, g * 16 + x * 4 + s] = 1
                norm_back[g * 16 + x * 4 + s, x * CHUNK + g * 4 + s] = 1
                source = (g % 8) * 8 + x * 2 + g // 8
                stash[x * CHUNK + g * 4 + s, source * 9 + s] = 1
            for j in range(OVER):
                for half in range(2):
                    over_out[half, g * 5 + j, g * 16 + half * 8 + j] = 1
                    over_back[half, g * 16 + half * 8 + j, x * CHUNK + 64 + g * 5 + j] = 1
                stash[x * CHUNK + 64 + g * 5 + j, source * 9 + 4 + j] = 1
    return [a.astype(jnp.bfloat16) for a in (norm_out, over_out, norm_back, over_back, stash)]


def dot(a, b):
    return jnp.dot(a, b, preferred_element_type=jnp.float32)


def dot_t(a, b):
    return lax.dot_general(a, b, (((1,), (1,)), ((), ())), preferred_element_type=jnp.float32)


def sigmoid(v):
    return 1.0 / (1.0 + jnp.exp(-v))


def route_ranks(route):
    lane = lax.broadcasted_iota(jnp.int32, (16, 128), 1)
    first = route[:, 0:1]
    second = route[:, 1:2]
    hits = jnp.where(first == lane, 1.0, 0.0) + jnp.where(second == lane, 1.0, 0.0)
    row = lax.broadcasted_iota(jnp.int32, (16, 16), 0)
    col = lax.broadcasted_iota(jnp.int32, (16, 16), 1)
    earlier = jnp.where(col < row, 1.0, 0.0).astype(jnp.bfloat16)
    before = dot(earlier, hits.astype(jnp.bfloat16))
    ranks = []
    for pick in (first, second):
        rank = jnp.sum(jnp.where(pick == lane, before, 0.0), axis=1, keepdims=True)
        ranks.append(rank.astype(jnp.int32))
    return ranks, jnp.sum(hits, axis=0, keepdims=True)


def choice_match(route, ranks, half=None):
    col = lax.broadcasted_iota(jnp.int32, (16, 128), 1)
    is_norm = col < 32
    expert = ((col >> 2) & 3) * 2 + (col >> 4)
    slot = jnp.where(is_norm, col & 3, 4 + (col & 7))
    if half is not None:
        slot = jnp.where(is_norm | (((col >> 3) & 1) == half), slot, 99)
    slot = jnp.where(col < (48 if half is None else 64), slot, 99)
    out = []
    for k in range(2):
        pick = route[:, k : k + 1]
        out.append((slot == ranks[k]) & ((expert == pick) | jnp.logical_not(is_norm)))
    return out


def gate_parts(route, gates, ranks, half):
    match = choice_match(route, ranks, half)
    total = jnp.where(match[0], gates[:, 0:1], 0.0) + jnp.where(match[1], gates[:, 1:2], 0.0)
    total = total[:, :64]
    high = total.astype(jnp.bfloat16)
    rest = total - high.astype(jnp.float32)
    middle = rest.astype(jnp.bfloat16)
    low = (rest - middle.astype(jnp.float32)).astype(jnp.bfloat16)
    return jnp.concatenate([high, middle, low], axis=0)


def kernel(
    x_f, r_f, g_f, x_b, r_b, g_b, wgu_h, wd_h, saved_h, p_no, p_oo, p_nb, p_ob, p_st,
    out_f, out_b,
    wgu, wd, wgu_s, wd_s, saved, c_no, c_oo, c_nb, c_ob, c_st,
    zsend, zrecv, xsend, xrecv, xsib,
    own_f, own_b, rss_f, rss_b, rsr_f, rsr_b, hid, pre,
    oret, orecv, wsend, wrecv, comb,
    load_sem, wx_ss, wx_rs, z_ss, z_rs, x_ss, x_rs, c_ss, c_rs, rs_ss, rs_rs, ag_ss, ag_rs, as_ss, as_rs,
    o_ss, o_rs, w_ss, w_rs, y_ss, y_rs,
):
    pipe = lax.axis_index("pipe")
    expert = lax.axis_index("expert")
    y, h = pipe // 8, pipe % 8
    zl, core = h // 2, h % 2
    x, zh = expert // 2, expert % 2
    g = zh * 8 + h

    def ring_id(gg):
        return (y * 8 + gg % 8, x * 2 + gg // 8)

    def x_id(xx):
        return (pipe, xx * 2 + zh)

    def line_id(zz):
        return (y * 8 + zz * 2 + core, expert)

    sib_id = (pipe + 1 - 2 * core, expert)

    def remote(src, dst, ss, rs, dev):
        return pltpu.make_async_remote_copy(
            src_ref=src, dst_ref=dst, send_sem=ss, recv_sem=rs, device_id=dev, device_id_type=MESH
        )

    loads = [
        pltpu.make_async_copy(a, b, load_sem.at[i])
        for i, (a, b) in enumerate(
            ((p_no, c_no), (p_oo, c_oo), (wgu_h, wgu), (wd_h, wd), (saved_h, saved), (p_st, c_st), (p_nb, c_nb), (p_ob, c_ob))
        )
    ]
    for load in loads:
        load.start()

    barrier = pltpu.get_barrier_semaphore()
    peers = [ring_id((g + d) % ZN) for d in range(1, ZN)]
    peers += [x_id((x + d) % XN) for d in range(1, XN)]
    peers += [((pipe + 8) % 64, expert), ((pipe + 56) % 64, expert)]
    for peer in peers:
        pl.semaphore_signal(barrier, inc=1, device_id=peer, device_id_type=MESH)

    routing = []
    for t, (xin, r_ref) in enumerate(((x_f, r_f), (x_b, r_b))):
        route = r_ref[...]
        ranks, counts = route_ranks(route)
        match = choice_match(route, ranks)
        pick = jnp.where(match[0] | match[1], 1.0, 0.0)
        pick = jnp.concatenate([pick, jnp.zeros((112, 128), jnp.float32)], axis=0)
        pick = jnp.transpose(pick)[:48, :16].astype(jnp.bfloat16)
        lane = lax.broadcasted_iota(jnp.int32, (1, 128), 1)
        mine = jnp.sum(jnp.where(lane == expert, counts, 0.0), axis=1, keepdims=True)
        routing.append((route, ranks, mine))
        upper = lax.broadcasted_iota(jnp.int32, (16, 256), 0) < 8
        for b in range(8):
            rows = dot(pick, xin[:, b * 512 : (b + 1) * 512]).astype(jnp.float32)
            over = jnp.where(upper, rows[32:48, :256], rows[32:48, 256:]).astype(jnp.bfloat16)
            for hi in range(2):
                zsend[t, hi * 8 + b, :, 0:512] = rows[hi * 16 : hi * 16 + 16].astype(jnp.bfloat16)
                zsend[t, hi * 8 + b, :, 512:768] = over

    pl.semaphore_wait(barrier, len(peers))

    def z_copy(t, d):
        to = (g + d) % ZN
        return remote(zsend.at[t, to], zrecv.at[t, g], z_ss.at[t, d], z_rs.at[t, d], ring_id(to))

    for t in range(2):
        for d in range(1, ZN):
            z_copy(t, d).start()
        zrecv[t, g] = zsend[t, g]

    wx = [
        remote(wgu_h.at[:, :, 1 - core], wgu_s, wx_ss.at[0], wx_rs.at[0], sib_id),
        remote(wd_h.at[:, 1 - core], wd_s, wx_ss.at[1], wx_rs.at[1], sib_id),
    ]
    for copy in wx:
        copy.start()
    loads[0].wait()
    loads[1].wait()

    def x_copy(t, d):
        to = (x + d) % XN
        return remote(xsend.at[t, to], xrecv.at[t, x], x_ss.at[t, d], x_rs.at[t, d], x_id(to))

    def chunk_of(i):
        return (x + XN - i) % XN

    def c_copy(t, i):
        at = chunk_of(i)
        return remote(xrecv.at[t, at], xsib.at[t, at], c_ss.at[t, i], c_rs.at[t, i], sib_id)

    for t in range(2):
        for d in range(1, ZN):
            z_copy(t, d).wait_recv()
        got = zrecv[t].reshape(256, 768)
        norm = dot(c_no[...], got[:, :512]).astype(jnp.bfloat16)
        over = jnp.concatenate(
            [dot(c_oo[0], got[:, 512:]), dot(c_oo[1], got[:, 512:])], axis=1
        ).astype(jnp.bfloat16)
        for xx in range(XN):
            xsend[t, xx, 0:64] = norm[xx * 64 : xx * 64 + 64]
            xsend[t, xx, 64:CHUNK] = over
        for d in range(1, XN):
            x_copy(t, d).start()
        xrecv[t, x] = xsend[t, x]
        c_copy(t, 0).start()

    for i in range(1, XN):
        for t in range(2):
            x_copy(t, i).wait_recv()
            c_copy(t, i).start()

    for load in loads[2:]:
        load.wait()
    for copy in wx:
        copy.wait_recv()

    rss = (rss_f, rss_b)
    rsr = (rsr_f, rsr_b)
    owns = (own_f, own_b)

    def rs_copy(t, d, i):
        return remote(
            rss[t].at[i, d], rsr[t].at[i, d], rs_ss.at[t, i, d], rs_rs.at[t, i, d], line_id((zl + d) % LINE)
        )

    for i in range(XN):
        at = chunk_of(i)
        for t in range(2):
            c_copy(t, i).wait_recv()
            mine = xrecv[t, at]
            other = xsib[t, at]
            for d in (2, 1, 3, 0):
                to = (zl + d) % LINE
                if t == 0:
                    w_mine = jnp.concatenate([wgu[0, to, core], wgu[1, to, core]], axis=0)
                    w_other = jnp.concatenate([wgu_s[0, to], wgu_s[1, to]], axis=0)
                else:
                    w_mine = wd[to, core]
                    w_other = wd_s[to]
                part = dot_t(mine, w_mine) + dot_t(other, w_other)
                if d == 0:
                    owns[t][i] = part
                else:
                    rss[t][i, d] = part.astype(jnp.bfloat16)
                    rs_copy(t, d, i).start()

    full = (hid, pre)

    def lanes(block):
        return pl.ds(pl.multiple_of(block * 128, 128), 128)

    def ag_copy(t, d, i):
        here = full[t].at[i, :, :, lanes(h)]
        return remote(here, here, ag_ss.at[t, i, d], ag_rs.at[t, i, d], line_id((zl + d) % LINE))

    def as_copy(t, d, i):
        block = ((zl + LINE - d) % LINE) * 2 + core
        here = full[t].at[i, :, :, lanes(block)]
        return remote(here, here, as_ss.at[t, i, d], as_rs.at[t, i, d], sib_id)

    for i in range(XN):
        at = chunk_of(i)
        for t in range(2):
            total = owns[t][i]
            for d in range(1, LINE):
                rs_copy(t, d, i).wait_recv()
                total = total + rsr[t][i, d].astype(jnp.float32)
            if t == 0:
                gate, up = total[:, :128], total[:, 128:]
                hid[i, 0, :, lanes(h)] = (gate * sigmoid(gate) * up).astype(jnp.bfloat16)
            else:
                kept = dot(c_st[pl.ds(pl.multiple_of(at * CHUNK, CHUNK), CHUNK), :], saved[...])
                gate, up = kept[:, :128], kept[:, 128:]
                sig = sigmoid(gate)
                pre[i, 0, :, lanes(h)] = (total * up * (sig * (1.0 + gate * (1.0 - sig)))).astype(jnp.bfloat16)
                pre[i, 1, :, lanes(h)] = (total * (gate * sig)).astype(jnp.bfloat16)
            for d in (2, 1, 3):
                ag_copy(t, d, i).start()
            as_copy(t, 0, i).start()

    for i in range(XN):
        for t in range(2):
            for d in range(1, LINE):
                ag_copy(t, d, i).wait_recv()
                as_copy(t, d, i).start()

    def o_copy(t, i):
        to = chunk_of(i)
        return remote(oret.at[t, to], orecv.at[t, x], o_ss.at[t, i], o_rs.at[t, i], x_id(to))

    wgu_flat = wgu.reshape(2, 1024, 512)
    wd_flat = wd.reshape(1024, 512)
    row = lax.broadcasted_iota(jnp.int32, (CHUNK, 512), 0)
    for i in (1, 2, 3, 0):
        at = chunk_of(i)
        for t in range(2):
            for d in range(LINE):
                as_copy(t, d, i).wait_recv()
            if t == 0:
                made = dot(hid[i, 0], wd_flat[...])
            else:
                made = dot(pre[i, 0], wgu_flat[0]) + dot(pre[i, 1], wgu_flat[1])
            made = jnp.where((row < 64) | (routing[t][2] > 4.5), made, 0.0).astype(jnp.bfloat16)
            if i == 0:
                orecv[t, x] = made
            else:
                oret[t, at] = made
                o_copy(t, i).start()

    def w_copy(t, d):
        to = (g + d) % ZN
        return remote(wsend.at[t, to], wrecv.at[t, g], w_ss.at[t, d], w_rs.at[t, d], ring_id(to))

    for t in range(2):
        for i in range(1, XN):
            o_copy(t, i).wait_recv()
        got = orecv[t].reshape(XN * CHUNK, 512)
        wsend[t, :, :, 0:512] = dot(c_nb[...], got).astype(jnp.bfloat16).reshape(ZN, 16, 512)
        over = dot(c_ob[0], got[:, :256]) + dot(c_ob[1], got[:, 256:])
        wsend[t, :, :, 512:768] = over.astype(jnp.bfloat16).reshape(ZN, 16, 256)
        for d in range(1, ZN):
            w_copy(t, d).start()
        wrecv[t, g] = wsend[t, g]

    ends = (((pipe + 8) % 64, expert), ((pipe + 56) % 64, expert))
    outs = (out_f, out_b)

    def y_copy(t):
        return remote(comb.at[t], outs[t], y_ss.at[t], y_rs.at[t], ends[t])

    for t, gates in enumerate((g_f, g_b)):
        route, ranks, _ = routing[t]
        parts = [gate_parts(route, gates[...], ranks, half) for half in range(2)]
        for d in range(1, ZN):
            w_copy(t, d).wait_recv()
        for b in range(8):
            for half in range(2):
                lo = half * 256
                rows = jnp.concatenate(
                    [
                        wrecv[t, b, :, lo : lo + 256],
                        wrecv[t, 8 + b, :, lo : lo + 256],
                        wrecv[t, b, :, 512:768],
                        wrecv[t, 8 + b, :, 512:768],
                    ],
                    axis=0,
                )
                mixed = dot(parts[half], rows)
                mixed = mixed[0:16] + mixed[16:32] + mixed[32:48]
                comb[t, :, b * 512 + lo : b * 512 + lo + 256] = mixed.astype(jnp.bfloat16)
        y_copy(t).start()

    for copy in wx:
        copy.wait_send()
    for t in range(2):
        for d in range(1, ZN):
            z_copy(t, d).wait_send()
            w_copy(t, d).wait_send()
        for d in range(1, XN):
            x_copy(t, d).wait_send()
            o_copy(t, d).wait_send()
        for i in range(XN):
            c_copy(t, i).wait_send()
            as_copy(t, 0, i).wait_send()
            for d in range(1, LINE):
                rs_copy(t, d, i).wait_send()
                ag_copy(t, d, i).wait_send()
                as_copy(t, d, i).wait_send()
    for t in range(2):
        y_copy(t).wait()


def on_device(x_f, r_f, g_f, x_b, r_b, g_b, gate_up, down, saved):
    vmem = pl.BlockSpec(memory_space=pltpu.VMEM)
    anywhere = pl.BlockSpec(memory_space=pl.ANY)
    bf16, f32 = jnp.bfloat16, jnp.float32
    dma = pltpu.SemaphoreType.DMA
    consts = [jnp.asarray(a) for a in permutations()]
    out = jax.ShapeDtypeStruct((16, 4096), bf16)
    scratch = [
        pltpu.VMEM((2, 4, 2, 128, 512), bf16),
        pltpu.VMEM((4, 2, 128, 512), bf16),
        pltpu.VMEM((2, 4, 128, 512), bf16),
        pltpu.VMEM((4, 128, 512), bf16),
        pltpu.VMEM((576, 256), bf16),
    ]
    scratch += [pltpu.VMEM(c.shape, bf16) for c in consts]
    scratch += [
        pltpu.VMEM((2, ZN, 16, 768), bf16),
        pltpu.VMEM((2, ZN, 16, 768), bf16),
        pltpu.VMEM((2, XN, CHUNK, 512), bf16),
        pltpu.VMEM((2, XN, CHUNK, 512), bf16),
        pltpu.VMEM((2, XN, CHUNK, 512), bf16),
        pltpu.VMEM((XN, CHUNK, 256), f32),
        pltpu.VMEM((XN, CHUNK, 128), f32),
        pltpu.VMEM((XN, LINE, CHUNK, 256), bf16),
        pltpu.VMEM((XN, LINE, CHUNK, 128), bf16),
        pltpu.VMEM((XN, LINE, CHUNK, 256), bf16),
        pltpu.VMEM((XN, LINE, CHUNK, 128), bf16),
        pltpu.VMEM((XN, 1, CHUNK, 1024), bf16),
        pltpu.VMEM((XN, 2, CHUNK, 1024), bf16),
        pltpu.VMEM((2, XN, CHUNK, 512), bf16),
        pltpu.VMEM((2, XN, CHUNK, 512), bf16),
        pltpu.VMEM((2, ZN, 16, 768), bf16),
        pltpu.VMEM((2, ZN, 16, 768), bf16),
        pltpu.VMEM((2, 16, 4096), bf16),
    ]
    scratch += [dma((8,)), dma((2,)), dma((2,))]
    scratch += [dma((2, ZN)), dma((2, ZN)), dma((2, XN)), dma((2, XN)), dma((2, XN)), dma((2, XN))]
    scratch += [dma((2, XN, LINE))] * 6
    scratch += [dma((2, XN)), dma((2, XN)), dma((2, ZN)), dma((2, ZN)), dma((2,)), dma((2,))]
    call = pl.pallas_call(
        kernel,
        out_shape=[out, out],
        in_specs=[vmem] * 6 + [anywhere] * 8,
        out_specs=[anywhere, anywhere],
        scratch_shapes=scratch,
        compiler_params=pltpu.CompilerParams(
            collective_id=0, has_side_effects=True, vmem_limit_bytes=48 * 1024 * 1024
        ),
        cost_estimate=pl.CostEstimate(flops=4 * 10**9, bytes_accessed=8 * 10**6, transcendentals=10**6),
    )
    next_input, prior_gradient = call(
        x_f[0], r_f[0], g_f[0], x_b[0], r_b[0], g_b[0],
        gate_up.reshape(2, 4, 2, 128, 512), down.reshape(4, 2, 128, 512), saved[0, 0], *consts,
    )
    return next_input[None], prior_gradient[None]


def solution(mesh):
    row = P("pipe", "expert", None)
    wide = P("pipe", "expert", None, None)
    return jax.shard_map(
        on_device,
        mesh=mesh,
        in_specs=(row,) * 6 + (wide,) * 3,
        out_specs=(row, row),
        check_vma=False,
    )
```

```python
import jax
import jax.numpy as jnp
from jax import lax
from jax.experimental import pallas as pl
from jax.experimental.pallas import tpu as pltpu
from jax.sharding import PartitionSpec as P

GROUP = 8
BASE = 4
OVER = 5
ZN = 16
XN = 4
LINE = 4
NORM = ZN * BASE
LATE = ZN * OVER
CHUNK = NORM + LATE
PIECES = (0, 1, 2)
F, B = 0, 1
MESH = pl.DeviceIdType.MESH


def one_hot(target, width):
    col = lax.broadcasted_iota(jnp.int32, (target.shape[0], width), 1)
    return jnp.where(col == target, 1.0, 0.0).astype(jnp.bfloat16)


def fifth(v):
    return (v * 205) >> 10


def rows_of(count):
    return lax.broadcasted_iota(jnp.int32, (count, 1), 0)


def norm_out():
    r = rows_of(256)
    return one_hot(((r >> 2) & 15) * 16 + (r >> 6) * 4 + (r & 3), 256)


def norm_back():
    r = rows_of(256)
    return one_hot(((r >> 2) & 3) * 64 + (r >> 4) * 4 + (r & 3), 256)


def over_out(half):
    r = rows_of(80)
    g = fifth(r)
    return one_hot(g * 16 + half * 8 + r - 5 * g, 256)


def over_back(half):
    r = rows_of(256)
    j = r & 7
    want = jnp.where((((r >> 3) & 1) == half) & (j < OVER), (r >> 4) * 5 + j, -1)
    one = one_hot(want, 80)
    return jnp.concatenate([one] * XN, axis=1)


def stash_rows(x):
    r = rows_of(CHUNK)
    k = r - NORM
    is_norm = k < 0
    g = jnp.where(is_norm, r >> 2, fifth(k))
    slot = jnp.where(is_norm, r & 3, 4 + k - 5 * g)
    return one_hot(((g & 7) * 8 + x * 2 + (g >> 3)) * 9 + slot, XN * CHUNK)


def dot(a, b):
    return jnp.dot(a, b, preferred_element_type=jnp.float32)


def dot_t(a, b):
    return lax.dot_general(a, b, (((1,), (1,)), ((), ())), preferred_element_type=jnp.float32)


def sigmoid(v):
    return 1.0 / (1.0 + jnp.exp(-v))


def route_ranks(route):
    name = lax.broadcasted_iota(jnp.int32, (8, 16), 0)
    picks = [route[k : k + 1] for k in range(2)]
    hits = jnp.where(picks[0] == name, 1.0, 0.0) + jnp.where(picks[1] == name, 1.0, 0.0)
    row = lax.broadcasted_iota(jnp.int32, (16, 16), 0)
    col = lax.broadcasted_iota(jnp.int32, (16, 16), 1)
    earlier = jnp.where(row < col, 1.0, 0.0).astype(jnp.bfloat16)
    before = dot(hits.astype(jnp.bfloat16), earlier)
    ranks = [
        jnp.sum(jnp.where(pick == name, before, 0.0), axis=0, keepdims=True).astype(jnp.int32) for pick in picks
    ]
    return ranks, jnp.sum(hits, axis=1, keepdims=True)


def choice_match(route, ranks, rows, half=None):
    row = lax.broadcasted_iota(jnp.int32, (rows, 16), 0)
    is_norm = row < 32
    expert = ((row >> 2) & 3) * 2 + (row >> 4)
    slot = jnp.where(is_norm, row & 3, 4 + (row & 7))
    if half is not None:
        slot = jnp.where(is_norm | (((row >> 3) & 1) == half), slot, 99)
    return [
        (slot == ranks[k]) & ((expert == route[k : k + 1]) | jnp.logical_not(is_norm)) for k in range(2)
    ]


def gate_parts(route, gates, ranks, half):
    match = choice_match(route, ranks, 64, half)
    total = jnp.where(match[0], gates[0:1], 0.0) + jnp.where(match[1], gates[1:2], 0.0)
    total = jnp.concatenate([total, jnp.zeros((64, 16), jnp.float32)], axis=0)
    total = jnp.concatenate([total, jnp.zeros((128, 112), jnp.float32)], axis=1)
    total = jnp.transpose(total)[:16, :64]
    high = total.astype(jnp.bfloat16)
    rest = total - high.astype(jnp.float32)
    middle = rest.astype(jnp.bfloat16)
    low = (rest - middle.astype(jnp.float32)).astype(jnp.bfloat16)
    return jnp.concatenate([high, middle, low], axis=0)


def buffers():
    bf16, f32 = jnp.bfloat16, jnp.float32
    out = {
        "xin": pltpu.VMEM((2, 16, 4096), bf16),
        "r_v": pltpu.VMEM((2, 2, 16), jnp.int32),
        "g_v": pltpu.VMEM((2, 2, 16), f32),
        "wgu": pltpu.VMEM((2, 4, 2, 128, 512), bf16),
        "wd": pltpu.VMEM((4, 2, 128, 512), bf16),
        "wgu_s": pltpu.VMEM((2, 4, 128, 512), bf16),
        "wd_s": pltpu.VMEM((4, 128, 512), bf16),
        "saved": pltpu.VMEM((576, 256), bf16),
        "c_no": pltpu.VMEM((256, 256), bf16),
        "c_oo": pltpu.VMEM((2, 80, 256), bf16),
        "c_nb": pltpu.VMEM((256, 256), bf16),
        "c_ob": pltpu.VMEM((2, 256, XN * LATE), bf16),
        "kept": pltpu.VMEM((2, 2 * NORM, 256), f32),
        "kept_o": pltpu.VMEM((LATE, 256), f32),
        "sv_s": pltpu.VMEM((XN, LATE, 256), bf16),
        "sv_r": pltpu.VMEM((XN, LATE, 256), bf16),
        "zsend": pltpu.VMEM((2, ZN, 16, 768), bf16),
        "zrecv": pltpu.VMEM((2, ZN, 16, 768), bf16),
        "wsend": pltpu.VMEM((2, ZN, 16, 768), bf16),
        "wrecv": pltpu.VMEM((2, ZN, 16, 768), bf16),
        "xsend": pltpu.VMEM((2, XN, CHUNK, 512), bf16),
        "xrecv": pltpu.VMEM((2, XN, CHUNK, 512), bf16),
        "xsib": pltpu.VMEM((2, XN, CHUNK, 512), bf16),
        "oret": pltpu.VMEM((2, XN, CHUNK, 512), bf16),
        "orecv": pltpu.VMEM((2, XN, CHUNK, 512), bf16),
        "comb": pltpu.VMEM((2, 16, 4096), bf16),
    }
    for t in (F, B):
        units = 256 if t == F else 128
        parts = 1 if t == F else 2
        out[f"xr_s{t}"] = pltpu.VMEM((XN, 4, LATE, units), bf16)
        out[f"xr_r{t}"] = pltpu.VMEM((XN, 4, LATE, units), bf16)
        for kind, count, rows in (("n", 2, 2 * NORM), ("o", 1, LATE)):
            out[f"own{t}{kind}"] = pltpu.VMEM((count, 4, rows, units), f32)
            out[f"tot{t}{kind}"] = pltpu.VMEM((count, rows, units), f32)
            for name, dests in (("ra", 3), ("rb", 2), ("rc", 1)):
                for way in "sr":
                    out[f"{name}_{way}{t}{kind}"] = pltpu.VMEM((count, dests, rows, units), bf16)
        out[f"hid{t}n"] = pltpu.VMEM((2, 2, parts, 2 * NORM, 512), bf16)
        out[f"hid{t}o"] = pltpu.VMEM((XN, 2, parts, LATE, 512), bf16)
    dma = pltpu.SemaphoreType.DMA
    out["load_sem"] = dma((9,))
    out["wx_sem"] = dma((2, 2))
    for name in ("z", "w"):
        out[name + "_sem"] = dma((2, 2, ZN))
    for name in ("x", "c", "xr", "xg", "xa", "on", "oo"):
        out[name + "_sem"] = dma((2, 2, XN))
    out["sv_sem"] = dma((2, XN))
    for name in ("ra", "rb", "rc", "as"):
        out[name + "_sem"] = dma((2, 2, 3))
    out["ag_ss"] = dma((2, 3, 5))
    out["ag_rs"] = dma((2, 3, LINE))
    out["y_sem"] = dma((2, 2))
    return out


def kernel(x_f, r_f, g_f, x_b, r_b, g_b, wgu_h, wd_h, saved_h, out_f, out_b, *scratch):
    s = dict(zip(buffers(), scratch))
    xin, r_v, g_v = s["xin"], s["r_v"], s["g_v"]
    wgu, wd, wgu_s, wd_s = s["wgu"], s["wd"], s["wgu_s"], s["wd_s"]
    zsend, zrecv, wsend, wrecv = s["zsend"], s["zrecv"], s["wsend"], s["wrecv"]
    xsend, xrecv, xsib, oret, orecv = s["xsend"], s["xrecv"], s["xsib"], s["oret"], s["orecv"]
    comb, kept, kept_o = s["comb"], s["kept"], s["kept_o"]

    pipe = lax.axis_index("pipe")
    expert = lax.axis_index("expert")
    y, h = pipe // 8, pipe % 8
    zl, core = h // 2, h % 2
    x, zh = expert // 2, expert % 2
    g = zh * 8 + h
    side = zl // 2
    is_end = zl % 3 == 0
    is_mid = zl % 3 != 0
    ne, nm, fm, fe = 3 * side, 1 + side, 2 - side, 3 - 3 * side

    def ring_id(gg):
        return (y * 8 + gg % 8, x * 2 + gg // 8)

    def x_id(xx):
        return (pipe, xx * 2 + zh)

    def line_id(zz):
        return (y * 8 + zz * 2 + core, expert)

    def chunk_of(i):
        return (x + XN - i) % XN

    sib_id = (pipe + 1 - 2 * core, expert)
    ends = (((pipe + 8) % 64, expert), ((pipe + 56) % 64, expert))

    def remote(src, dst, ss, rs, dev):
        return pltpu.make_async_remote_copy(
            src_ref=src, dst_ref=dst, send_sem=ss, recv_sem=rs, device_id=dev, device_id_type=MESH
        )

    def pair(name, *at):
        sem = s[name + "_sem"]
        return sem.at[(0,) + at], sem.at[(1,) + at]

    def piece(name, t, q):
        return s[f"{name}{t}n"].at[q] if q < 2 else s[f"{name}{t}o"].at[0]

    def full(t, q):
        return s[f"hid{t}n"].at[q] if q < 2 else s[f"hid{t}o"].at[x]

    def block_at(zz):
        return pl.ds(pl.multiple_of(zz * 128, 128), 128)

    def z_copy(t, d):
        to = (g + d) % ZN
        return remote(zsend.at[t, to], zrecv.at[t, g], *pair("z", t, d), ring_id(to))

    def x_copy(t, d):
        to = (x + d) % XN
        return remote(xsend.at[t, to], xrecv.at[t, x], *pair("x", t, d), x_id(to))

    def c_copy(t, i):
        at = chunk_of(i)
        return remote(xrecv.at[t, at], xsib.at[t, at], *pair("c", t, i), sib_id)

    def sv_copy(i):
        return remote(s["sv_s"].at[i], s["sv_r"].at[i], *pair("sv", i), x_id(chunk_of(i)))

    def xr_copy(t, i):
        return remote(s[f"xr_s{t}"].at[i], s[f"xr_r{t}"].at[i], *pair("xr", t, i), x_id(chunk_of(i)))

    def r_copy(name, t, q):
        to = {"ra": nm, "rb": fm, "rc": ne}[name]
        return remote(piece(name + "_s", t, q), piece(name + "_r", t, q), *pair(name, t, q), line_id(to))

    def ag_copy(t, q, block, to, k):
        here = full(t, q).at[core, :, :, block_at(block)]
        return remote(here, here, s["ag_ss"].at[t, q, k], s["ag_rs"].at[t, q, block], line_id(to))

    def as_copy(t, q):
        here = full(t, q).at[core]
        return remote(here, here, *pair("as", t, q), sib_id)

    def xg_copy(t, i):
        here = s[f"hid{t}o"].at[x, core]
        return remote(here, here, *pair("xg", t, i), x_id((x + i) % XN))

    def xa_copy(t, i):
        here = s[f"hid{t}o"].at[chunk_of(i), core]
        return remote(here, here, *pair("xa", t, i), sib_id)

    def on_copy(t, i):
        rows, to = pl.ds(0, NORM), chunk_of(i)
        return remote(oret.at[t, to, rows], orecv.at[t, x, rows], *pair("on", t, i), x_id(to))

    def oo_copy(t, i):
        rows, to = pl.ds(NORM, LATE), chunk_of(i)
        return remote(oret.at[t, to, rows], orecv.at[t, x, rows], *pair("oo", t, i), x_id(to))

    def w_copy(t, d):
        to = (g + d) % ZN
        return remote(wsend.at[t, to], wrecv.at[t, g], *pair("w", t, d), ring_id(to))

    def y_copy(t):
        return remote(comb.at[t], (out_f, out_b)[t], *pair("y", t), ends[t])

    wx = [
        remote(wgu_h.at[:, :, 1 - core], wgu_s, *pair("wx", 0), sib_id),
        remote(wd_h.at[:, 1 - core], wd_s, *pair("wx", 1), sib_id),
    ]

    moves = (
        (r_b, r_v.at[B]), (x_b, xin.at[B]), (r_f, r_v.at[F]), (x_f, xin.at[F]), (g_f, g_v.at[F]), (g_b, g_v.at[B]),
        (saved_h, s["saved"]), (wgu_h, wgu), (wd_h, wd),
    )
    loads = [pltpu.make_async_copy(a, b, s["load_sem"].at[i]) for i, (a, b) in enumerate(moves)]
    for load in loads:
        load.start()

    barrier = pltpu.get_barrier_semaphore()
    peers = [ring_id((g + d) % ZN) for d in range(1, ZN)]
    peers += [x_id((x + d) % XN) for d in range(1, XN)]
    peers += list(ends)
    for peer in peers:
        pl.semaphore_signal(barrier, inc=1, device_id=peer, device_id_type=MESH)

    for load in loads[:6]:
        load.wait()
    routing = {}
    for t in (B, F):
        route = r_v[t]
        ranks, counts = route_ranks(route)
        match = choice_match(route, ranks, 48)
        pick = jnp.where(match[0] | match[1], 1.0, 0.0).astype(jnp.bfloat16)
        name = lax.broadcasted_iota(jnp.int32, (8, 1), 0)
        mine = jnp.sum(jnp.where(name == expert, counts, 0.0), axis=0, keepdims=True)
        routing[t] = (route, ranks, mine > BASE + 0.5)
        upper = lax.broadcasted_iota(jnp.int32, (16, 256), 0) < 8
        for b in range(8):
            rows = dot(pick, xin[t, :, b * 512 : (b + 1) * 512])
            over = jnp.where(upper, rows[32:48, :256], rows[32:48, 256:]).astype(jnp.bfloat16)
            for hi in range(2):
                zsend[t, hi * 8 + b, :, 0:512] = rows[hi * 16 : hi * 16 + 16].astype(jnp.bfloat16)
                zsend[t, hi * 8 + b, :, 512:768] = over

    def busiest_only(t, value):
        return jnp.where(routing[t][2], value, 0.0)

    pl.semaphore_wait(barrier, len(peers))

    for t in (B, F):
        for d in range(1, ZN):
            z_copy(t, d).start()
        zrecv[t, g] = zsend[t, g]
    for copy in wx:
        copy.start()

    s["c_no"][...] = norm_out()
    s["c_nb"][...] = norm_back()
    for half in range(2):
        s["c_oo"][half] = over_out(half)
        s["c_ob"][half] = over_back(half)
    loads[6].wait()
    for i in range(XN):
        found = dot(stash_rows(chunk_of(i)), s["saved"][...])
        kept[i // 2, (i % 2) * NORM : (i % 2 + 1) * NORM] = found[:NORM]
        late = busiest_only(B, found[NORM:])
        if i == 0:
            kept_o[...] = late
        else:
            s["sv_s"][i] = late.astype(jnp.bfloat16)
            sv_copy(i).start()

    def rows_to_x(t):
        for d in range(1, ZN):
            z_copy(t, d).wait_recv()
        got = zrecv[t].reshape(256, 768)
        norm = dot(s["c_no"][...], got[:, :512]).astype(jnp.bfloat16)
        over = jnp.concatenate(
            [dot(s["c_oo"][0], got[:, 512:]), dot(s["c_oo"][1], got[:, 512:])], axis=1
        ).astype(jnp.bfloat16)
        for xx in range(XN):
            xsend[t, xx, 0:NORM] = norm[xx * NORM : (xx + 1) * NORM]
            xsend[t, xx, NORM:CHUNK] = over
        for d in range(1, XN):
            x_copy(t, d).start()
        xrecv[t, x] = xsend[t, x]
        c_copy(t, 0).start()

    def rows_to_sibling(t):
        for i in range(1, XN):
            x_copy(t, i).wait_recv()
            c_copy(t, i).start()

    def weights(t, dest):
        if t == F:
            return (
                jnp.concatenate([wgu[0, dest, core], wgu[1, dest, core]], axis=0),
                jnp.concatenate([wgu_s[0, dest], wgu_s[1, dest]], axis=0),
            )
        return wd[dest, core], wd_s[dest]

    def late_products(t):
        for i in (1, 2, 3, 0):
            c_copy(t, i).wait_recv()
            at = chunk_of(i)
            for k, dest in enumerate((fe, fm, nm, ne)):
                w_mine, w_other = weights(t, dest)
                part = dot_t(xrecv[t, at, NORM:], w_mine) + dot_t(xsib[t, at, NORM:], w_other)
                part = busiest_only(t, part)
                if i == 0:
                    s[f"own{t}o"][0, k] = part
                else:
                    s[f"xr_s{t}"][i, k] = part.astype(jnp.bfloat16)
            if i > 0:
                xr_copy(t, i).start()

    def norm_products(t):
        for q in range(2):
            ats = [chunk_of(2 * q), chunk_of(2 * q + 1)]
            mine = jnp.concatenate([xrecv[t, at, :NORM] for at in ats], axis=0)
            other = jnp.concatenate([xsib[t, at, :NORM] for at in ats], axis=0)
            for k, dest in enumerate((fe, fm, nm, ne)):
                w_mine, w_other = weights(t, dest)
                part = dot_t(mine, w_mine) + dot_t(other, w_other)
                s[f"own{t}n"][q, k] = part
                if k < 3:
                    s[f"ra_s{t}n"][q, k] = part.astype(jnp.bfloat16)
            ends_send(t, q)

    def ends_send(t, q):
        @pl.when(is_end)
        def _():
            r_copy("ra", t, q).start()

    def late_sum(t):
        for k in range(4):
            total = s[f"own{t}o"][0, k]
            for i in range(1, XN):
                if k == 0:
                    xr_copy(t, i).wait_recv()
                total = total + s[f"xr_r{t}"][i, k].astype(jnp.float32)
            s[f"own{t}o"][0, k] = total
            if k < 3:
                s[f"ra_s{t}o"][0, k] = total.astype(jnp.bfloat16)
        ends_send(t, 2)

    def middles_send(t, q):
        @pl.when(is_mid)
        def _():
            r_copy("ra", t, q).wait_recv()
            own, came = piece("own", t, q), piece("ra_r", t, q)
            for k in range(2):
                piece("rb_s", t, q)[k] = (own[k] + came[k].astype(jnp.float32)).astype(jnp.bfloat16)
            r_copy("rb", t, q).start()

    def middles_return(t, q):
        @pl.when(is_mid)
        def _():
            r_copy("rb", t, q).wait_recv()
            own, came = piece("own", t, q), piece("rb_r", t, q)
            piece("rc_s", t, q)[0] = (own[3] + came[0].astype(jnp.float32)).astype(jnp.bfloat16)
            r_copy("rc", t, q).start()
            near = piece("ra_r", t, q)
            piece("tot", t, q)[...] = own[2] + near[2].astype(jnp.float32) + came[1].astype(jnp.float32)

    def activate(t, q):
        @pl.when(is_end)
        def _():
            r_copy("rc", t, q).wait_recv()
            piece("tot", t, q)[...] = piece("own", t, q)[3] + piece("rc_r", t, q)[0].astype(jnp.float32)

        total = piece("tot", t, q)[...]
        hid = full(t, q)
        if t == F:
            gate, up = total[:, :128], total[:, 128:]
            hid[core, 0, :, block_at(zl)] = (gate * sigmoid(gate) * up).astype(jnp.bfloat16)
        else:
            stash = kept[q] if q < 2 else kept_o[...]
            gate, up = stash[:, :128], stash[:, 128:]
            sig = sigmoid(gate)
            slope = sig * (1.0 + gate * (1.0 - sig))
            hid[core, 0, :, block_at(zl)] = (total * up * slope).astype(jnp.bfloat16)
            hid[core, 1, :, block_at(zl)] = (total * (gate * sig)).astype(jnp.bfloat16)

        @pl.when(is_end)
        def _():
            ag_copy(t, q, ne, nm, 0).start()

        @pl.when(is_mid)
        def _():
            ag_copy(t, q, nm, fm, 1).start()
            ag_copy(t, q, nm, ne, 0).start()

    def relay_near(t, q):
        @pl.when(is_mid)
        def _():
            ag_copy(t, q, ne, nm, 0).wait_recv()
            ag_copy(t, q, ne, fm, 2).start()
            ag_copy(t, q, fm, nm, 0).wait_recv()
            ag_copy(t, q, fm, ne, 3).start()

    def relay_far(t, q):
        @pl.when(is_mid)
        def _():
            ag_copy(t, q, fe, nm, 0).wait_recv()
            ag_copy(t, q, fe, ne, 4).start()

    def units_to_sibling(t, q):
        @pl.when(is_end)
        def _():
            for block in (nm, fm, fe):
                ag_copy(t, q, block, ne, 0).wait_recv()

        as_copy(t, q).start()
        if q == 2:
            for i in range(1, XN):
                xg_copy(t, i).start()

    def down(t, hid):
        if t == F:
            return dot(hid[0, 0], wd[:, 0].reshape(512, 512)) + dot(hid[1, 0], wd[:, 1].reshape(512, 512))
        total = None
        for c in range(2):
            for a in range(2):
                part = dot(hid[c, a], wgu[a, :, c].reshape(512, 512))
                total = part if total is None else total + part
        return total

    def norm_back_to_x(t):
        for q in (1, 0):
            as_copy(t, q).wait_recv()
            made = down(t, s[f"hid{t}n"].at[q]).astype(jnp.bfloat16)
            for i in (2 * q + 1, 2 * q):
                rows = made[(i % 2) * NORM : (i % 2 + 1) * NORM]
                if i == 0:
                    orecv[t, x, 0:NORM] = rows
                else:
                    oret[t, chunk_of(i), 0:NORM] = rows
                    on_copy(t, i).start()

    def late_to_sibling(t):
        for i in range(1, XN):
            xg_copy(t, i).wait_recv()
            xa_copy(t, i).start()

    def late_back_to_x(t):
        for i in (1, 2, 3, 0):
            if i == 0:
                as_copy(t, 2).wait_recv()
            else:
                xa_copy(t, i).wait_recv()
            made = down(t, s[f"hid{t}o"].at[chunk_of(i)])
            made = busiest_only(t, made).astype(jnp.bfloat16)
            if i == 0:
                orecv[t, x, NORM:CHUNK] = made
            else:
                oret[t, chunk_of(i), NORM:CHUNK] = made
                oo_copy(t, i).start()

    def rows_to_sources(t):
        for i in range(1, XN):
            on_copy(t, i).wait_recv()
            oo_copy(t, i).wait_recv()
        norm = orecv[t, :, 0:NORM, :].reshape(XN * NORM, 512)
        wsend[t, :, :, 0:512] = dot(s["c_nb"][...], norm).astype(jnp.bfloat16).reshape(ZN, 16, 512)
        late = orecv[t, :, NORM:CHUNK, :].reshape(XN * LATE, 512)
        over = dot(s["c_ob"][0], late[:, :256]) + dot(s["c_ob"][1], late[:, 256:])
        wsend[t, :, :, 512:768] = over.astype(jnp.bfloat16).reshape(ZN, 16, 256)
        for d in range(1, ZN):
            w_copy(t, d).start()
        wrecv[t, g] = wsend[t, g]

    def combine(t):
        route, ranks, _ = routing[t]
        parts = [gate_parts(route, g_v[t], ranks, half) for half in range(2)]
        for d in range(1, ZN):
            w_copy(t, d).wait_recv()
        for b in range(8):
            for half in range(2):
                lo = half * 256
                rows = jnp.concatenate(
                    [
                        wrecv[t, b, :, lo : lo + 256],
                        wrecv[t, 8 + b, :, lo : lo + 256],
                        wrecv[t, b, :, 512:768],
                        wrecv[t, 8 + b, :, 512:768],
                    ],
                    axis=0,
                )
                mixed = dot(parts[half], rows)
                mixed = mixed[0:16] + mixed[16:32] + mixed[32:48]
                comb[t, :, b * 512 + lo : b * 512 + lo + 256] = mixed.astype(jnp.bfloat16)
        y_copy(t).start()

    rows_to_x(B)
    for load in loads[7:]:
        load.wait()
    for copy in wx:
        copy.wait_recv()
    rows_to_sibling(B)
    late_products(B)
    norm_products(B)
    rows_to_x(F)
    for i in range(1, XN):
        sv_copy(i).wait_recv()
        kept_o[...] += s["sv_r"][i].astype(jnp.float32)
    for q in range(2):
        middles_send(B, q)
    late_sum(B)
    rows_to_sibling(F)
    for q in range(2):
        middles_return(B, q)
    late_products(F)
    for q in range(2):
        activate(B, q)
    middles_send(B, 2)
    norm_products(F)
    for q in range(2):
        relay_near(B, q)
    middles_return(B, 2)
    for q in range(2):
        middles_send(F, q)
    for q in range(2):
        relay_far(B, q)
    activate(B, 2)
    late_sum(F)
    for q in range(2):
        units_to_sibling(B, q)
    for q in range(2):
        middles_return(F, q)
    relay_near(B, 2)
    norm_back_to_x(B)
    for q in range(2):
        activate(F, q)
    relay_far(B, 2)
    middles_send(F, 2)
    units_to_sibling(B, 2)
    for q in range(2):
        relay_near(F, q)
    middles_return(F, 2)
    late_to_sibling(B)
    for q in range(2):
        relay_far(F, q)
    activate(F, 2)
    late_back_to_x(B)
    for q in range(2):
        units_to_sibling(F, q)
    relay_near(F, 2)
    norm_back_to_x(F)
    relay_far(F, 2)
    rows_to_sources(B)
    units_to_sibling(F, 2)
    late_to_sibling(F)
    late_back_to_x(F)
    rows_to_sources(F)
    combine(B)
    combine(F)

    for copy in wx:
        copy.wait_send()
    for i in range(1, XN):
        sv_copy(i).wait_send()
    for t in (B, F):
        for d in range(1, ZN):
            z_copy(t, d).wait_send()
            w_copy(t, d).wait_send()
        for i in range(XN):
            c_copy(t, i).wait_send()
        for i in range(1, XN):
            for copy in (x_copy, xr_copy, xg_copy, xa_copy, on_copy, oo_copy):
                copy(t, i).wait_send()
        for q in PIECES:
            as_copy(t, q).wait_send()

        @pl.when(is_end)
        def _():
            for q in PIECES:
                r_copy("ra", t, q).wait_send()
                ag_copy(t, q, ne, nm, 0).wait_send()

        @pl.when(is_mid)
        def _():
            for q in PIECES:
                r_copy("rb", t, q).wait_send()
                r_copy("rc", t, q).wait_send()
                for k in range(5):
                    ag_copy(t, q, ne, ne, k).wait_send()

    for t in (B, F):
        y_copy(t).wait()


def on_device(x_f, r_f, g_f, x_b, r_b, g_b, gate_up, down, saved):
    in_hbm = pl.BlockSpec(memory_space=pltpu.HBM)
    out = jax.ShapeDtypeStruct((16, 4096), jnp.bfloat16)
    call = pl.pallas_call(
        kernel,
        out_shape=[out, out],
        in_specs=[in_hbm] * 9,
        out_specs=[in_hbm, in_hbm],
        scratch_shapes=list(buffers().values()),
        compiler_params=pltpu.CompilerParams(
            collective_id=0, has_side_effects=True, vmem_limit_bytes=60 * 1024 * 1024
        ),
        cost_estimate=pl.CostEstimate(flops=4 * 10**9, bytes_accessed=8 * 10**6, transcendentals=10**6),
    )
    next_input, prior_gradient = call(
        x_f[0], r_f[0].T, g_f[0].T, x_b[0], r_b[0].T, g_b[0].T,
        gate_up.reshape(2, 4, 2, 128, 512), down.reshape(4, 2, 128, 512), saved[0, 0],
    )
    return next_input[None], prior_gradient[None]


def solution(mesh):
    row = P("pipe", "expert", None)
    wide = P("pipe", "expert", None, None)
    return jax.shard_map(
        on_device,
        mesh=mesh,
        in_specs=(row,) * 6 + (wide,) * 3,
        out_specs=(row, row),
        check_vma=False,
    )
```

```python
import jax
import jax.numpy as jnp
from jax import lax
from jax.experimental import pallas as pl
from jax.experimental.pallas import tpu as pltpu
from jax.sharding import PartitionSpec as P

GROUP = 8
BASE = 4
OVER = 5
ZN = 16
XN = 4
LINE = 4
NORM = ZN * BASE
LATE = ZN * OVER
CHUNK = NORM + LATE
F, B = 0, 1
KINDS = {"n": NORM, "o": LATE}
WIDTH = {"n": 512, "o": 256}
STREAMS = ((B, "o"), (B, "n"), (F, "o"), (F, "n"))
Z_ORDER = (8, 7, 9, 6, 10, 5, 11, 4, 12, 3, 13, 2, 14, 1, 15)
LAG = (0, 1, 2, 3)
SHIFTS = (2, 1, 3, 0)
PIECES = {"n": 2, "o": 1}
MESH = pl.DeviceIdType.MESH


def one_hot(target, width):
    col = lax.broadcasted_iota(jnp.int32, (target.shape[0], width), 1)
    return jnp.where(col == target, 1.0, 0.0).astype(jnp.bfloat16)


def fifth(v):
    return (v * 205) >> 10


def rows_of(count):
    return lax.broadcasted_iota(jnp.int32, (count, 1), 0)


def norm_out():
    r = rows_of(256)
    return one_hot(((r >> 2) & 15) * 16 + (r >> 6) * 4 + (r & 3), 256)


def norm_back():
    r = rows_of(256)
    return one_hot(((r >> 2) & 3) * 64 + (r >> 4) * 4 + (r & 3), 256)


def over_out(half):
    r = rows_of(80)
    g = fifth(r)
    return one_hot(g * 16 + half * 8 + r - 5 * g, 256)


def over_back(half):
    r = rows_of(256)
    j = r & 7
    want = jnp.where((((r >> 3) & 1) == half) & (j < OVER), (r >> 4) * 5 + j, -1)
    one = one_hot(want, 80)
    return jnp.concatenate([one] * XN, axis=1)


def stash_rows(x):
    r = rows_of(CHUNK)
    k = r - NORM
    is_norm = k < 0
    g = jnp.where(is_norm, r >> 2, fifth(k))
    slot = jnp.where(is_norm, r & 3, 4 + k - 5 * g)
    return one_hot(((g & 7) * 8 + x * 2 + (g >> 3)) * 9 + slot, XN * CHUNK)


def dot(a, b):
    return jnp.dot(a, b, preferred_element_type=jnp.float32)


def dot_t(a, b):
    return lax.dot_general(a, b, (((1,), (1,)), ((), ())), preferred_element_type=jnp.float32)


def sigmoid(v):
    return 1.0 / (1.0 + jnp.exp(-v))


def route_ranks(route):
    name = lax.broadcasted_iota(jnp.int32, (8, 16), 0)
    picks = [route[k : k + 1] for k in range(2)]
    hits = jnp.where(picks[0] == name, 1.0, 0.0) + jnp.where(picks[1] == name, 1.0, 0.0)
    row = lax.broadcasted_iota(jnp.int32, (16, 16), 0)
    col = lax.broadcasted_iota(jnp.int32, (16, 16), 1)
    earlier = jnp.where(row < col, 1.0, 0.0).astype(jnp.bfloat16)
    before = dot(hits.astype(jnp.bfloat16), earlier)
    ranks = [
        jnp.sum(jnp.where(pick == name, before, 0.0), axis=0, keepdims=True).astype(jnp.int32) for pick in picks
    ]
    return ranks, jnp.sum(hits, axis=1, keepdims=True)


def choice_match(route, ranks, rows, half=None):
    row = lax.broadcasted_iota(jnp.int32, (rows, 16), 0)
    is_norm = row < 32
    expert = ((row >> 2) & 3) * 2 + (row >> 4)
    slot = jnp.where(is_norm, row & 3, 4 + (row & 7))
    if half is not None:
        slot = jnp.where(is_norm | (((row >> 3) & 1) == half), slot, 99)
    return [
        (slot == ranks[k]) & ((expert == route[k : k + 1]) | jnp.logical_not(is_norm)) for k in range(2)
    ]


def gate_parts(route, gates, ranks, half):
    match = choice_match(route, ranks, 64, half)
    total = jnp.where(match[0], gates[0:1], 0.0) + jnp.where(match[1], gates[1:2], 0.0)
    total = jnp.concatenate([total, jnp.zeros((64, 16), jnp.float32)], axis=0)
    total = jnp.concatenate([total, jnp.zeros((128, 112), jnp.float32)], axis=1)
    total = jnp.transpose(total)[:16, :64]
    high = total.astype(jnp.bfloat16)
    rest = total - high.astype(jnp.float32)
    middle = rest.astype(jnp.bfloat16)
    low = (rest - middle.astype(jnp.float32)).astype(jnp.bfloat16)
    return jnp.concatenate([high, middle, low], axis=0)


def buffers():
    bf16, f32 = jnp.bfloat16, jnp.float32
    out = {
        "xin": pltpu.VMEM((2, 16, 4096), bf16),
        "r_v": pltpu.VMEM((2, 2, 16), jnp.int32),
        "g_v": pltpu.VMEM((2, 2, 16), f32),
        "wgu": pltpu.VMEM((2, 4, 2, 128, 512), bf16),
        "wd": pltpu.VMEM((4, 2, 128, 512), bf16),
        "wgu_s": pltpu.VMEM((2, 4, 128, 512), bf16),
        "wd_s": pltpu.VMEM((4, 128, 512), bf16),
        "up_f": pltpu.VMEM((2, 512, 4 * 256), bf16),
        "up_b": pltpu.VMEM((2, 512, 4 * 128), bf16),
        "saved": pltpu.VMEM((576, 256), bf16),
        "c_no": pltpu.VMEM((256, 256), bf16),
        "c_oo": pltpu.VMEM((2, 80, 256), bf16),
        "c_nb": pltpu.VMEM((256, 256), bf16),
        "c_ob": pltpu.VMEM((2, 256, XN * LATE), bf16),
        "kept_n": pltpu.VMEM((2, 2 * NORM, 256), f32),
        "kept_o": pltpu.VMEM((1, LATE, 256), f32),
        "sv_s": pltpu.VMEM((XN, LATE, 256), bf16),
        "sv_r": pltpu.VMEM((XN, LATE, 256), bf16),
        "mix": pltpu.VMEM((2, 16, 4096), f32),
        "comb": pltpu.VMEM((2, 16, 4096), bf16),
    }
    for kind, rows in KINDS.items():
        for name in ("zsend", "zrecv", "wsend", "wrecv"):
            out[name + kind] = pltpu.VMEM((2, ZN, 16, WIDTH[kind]), bf16)
        for name in ("xsend", "xrecv", "xsib", "oret", "orecv"):
            out[name + kind] = pltpu.VMEM((2, XN, rows, 512), bf16)
    for t in (F, B):
        units = 256 if t == F else 128
        parts = 1 if t == F else 2
        out[f"xr_own{t}"] = pltpu.VMEM((4, LATE, units), f32)
        out[f"xr_s{t}"] = pltpu.VMEM((XN, 4, LATE, units), bf16)
        out[f"xr_r{t}"] = pltpu.VMEM((XN, 4, LATE, units), bf16)
        for kind, rows in (("n", 2 * NORM), ("o", LATE)):
            out[f"own{t}{kind}"] = pltpu.VMEM((PIECES[kind], rows, units), f32)
            for way in "sr":
                out[f"rs_{way}{t}{kind}"] = pltpu.VMEM((PIECES[kind], 3, rows, units), bf16)
            count = 2 if kind == "n" else XN
            out[f"hid{t}{kind}"] = pltpu.VMEM((count, 2, parts, rows, 512), bf16)
    dma = pltpu.SemaphoreType.DMA
    out["load_sem"] = dma((9,))
    out["wx_sem"] = dma((2, 2))
    for kind in KINDS:
        for name in ("z", "w"):
            out[name + kind + "_sem"] = dma((2, 2, ZN))
        for name in ("x", "c", "b"):
            out[name + kind + "_sem"] = dma((2, 2, XN))
        out["as" + kind + "_sem"] = dma((2, 2, PIECES[kind]))
        for name in ("rs", "ag"):
            out[name + kind + "_sem"] = dma((2, 2, PIECES[kind], 3))
    for name in ("xr", "xg", "xa"):
        out[name + "_sem"] = dma((2, 2, XN))
    out["sv_sem"] = dma((2, XN))
    out["y_sem"] = dma((2, 2))
    return out


def kernel(x_f, r_f, g_f, x_b, r_b, g_b, wgu_h, wd_h, saved_h, out_f, out_b, *scratch):
    s = dict(zip(buffers(), scratch))
    xin, r_v, g_v = s["xin"], s["r_v"], s["g_v"]
    wgu, wd, wgu_s, wd_s = s["wgu"], s["wd"], s["wgu_s"], s["wd_s"]
    comb, mix = s["comb"], s["mix"]

    pipe = lax.axis_index("pipe")
    expert = lax.axis_index("expert")
    y, h = pipe // 8, pipe % 8
    zl, core = h // 2, h % 2
    x, zh = expert // 2, expert % 2
    g = zh * 8 + h
    def ring_id(gg):
        return (y * 8 + gg % 8, x * 2 + gg // 8)

    def x_id(xx):
        return (pipe, xx * 2 + zh)

    def line_id(zz):
        return (y * 8 + zz * 2 + core, expert)

    def chunk_of(i):
        return (x + XN - i) % XN

    sib_id = (pipe + 1 - 2 * core, expert)
    ends = (((pipe + 8) % 64, expert), ((pipe + 56) % 64, expert))

    def remote(src, dst, ss, rs, dev):
        return pltpu.make_async_remote_copy(
            src_ref=src, dst_ref=dst, send_sem=ss, recv_sem=rs, device_id=dev, device_id_type=MESH
        )

    def pair(name, *at):
        sem = s[name + "_sem"]
        return sem.at[(0,) + at], sem.at[(1,) + at]

    def piece(name, st, q):
        return s[f"{name}{st[0]}{st[1]}"].at[q]

    def block_at(zz):
        return pl.ds(pl.multiple_of(zz * 128, 128), 128)

    def z_copy(st, d):
        t, kind = st
        to = (g + d) % ZN
        return remote(s["zsend" + kind].at[t, to], s["zrecv" + kind].at[t, g], *pair("z" + kind, t, d), ring_id(to))

    def x_copy(st, d):
        t, kind = st
        to = (x + d) % XN
        return remote(s["xsend" + kind].at[t, to], s["xrecv" + kind].at[t, x], *pair("x" + kind, t, d), x_id(to))

    def c_copy(st, i):
        t, kind = st
        at = chunk_of(i)
        return remote(s["xrecv" + kind].at[t, at], s["xsib" + kind].at[t, at], *pair("c" + kind, t, i), sib_id)

    def units_of(st, q):
        return piece("hid", st, q if st[1] == "n" else x)

    def sv_copy(i):
        return remote(s["sv_s"].at[i], s["sv_r"].at[i], *pair("sv", i), x_id(chunk_of(i)))

    def xr_copy(t, i):
        return remote(s[f"xr_s{t}"].at[i], s[f"xr_r{t}"].at[i], *pair("xr", t, i), x_id(chunk_of(i)))

    def rs_copy(st, q, k):
        src, dst = piece("rs_s", st, q).at[k], piece("rs_r", st, q).at[k]
        return remote(src, dst, *pair("rs" + st[1], st[0], q, k), line_id((zl + SHIFTS[k]) % LINE))

    def ag_copy(st, q, k):
        here = units_of(st, q).at[core, :, :, block_at(zl)]
        return remote(here, here, *pair("ag" + st[1], st[0], q, k), line_id((zl + SHIFTS[k]) % LINE))

    def as_copy(st, q):
        here = units_of(st, q).at[core]
        return remote(here, here, *pair("as" + st[1], st[0], q), sib_id)

    def xg_copy(t, i):
        here = s[f"hid{t}o"].at[x, core]
        return remote(here, here, *pair("xg", t, i), x_id((x + i) % XN))

    def xa_copy(t, i):
        here = s[f"hid{t}o"].at[chunk_of(i), core]
        return remote(here, here, *pair("xa", t, i), sib_id)

    def b_copy(st, i):
        t, kind = st
        to = chunk_of(i)
        return remote(s["oret" + kind].at[t, to], s["orecv" + kind].at[t, x], *pair("b" + kind, t, i), x_id(to))

    def w_copy(st, d):
        t, kind = st
        to = (g + d) % ZN
        return remote(s["wsend" + kind].at[t, to], s["wrecv" + kind].at[t, g], *pair("w" + kind, t, d), ring_id(to))

    def y_copy(t):
        return remote(comb.at[t], (out_f, out_b)[t], *pair("y", t), ends[t])

    wx = [
        remote(wgu_h.at[:, :, 1 - core], wgu_s, *pair("wx", 0), sib_id),
        remote(wd_h.at[:, 1 - core], wd_s, *pair("wx", 1), sib_id),
    ]

    moves = (
        (r_b, r_v.at[B]), (x_b, xin.at[B]), (r_f, r_v.at[F]), (x_f, xin.at[F]), (g_f, g_v.at[F]), (g_b, g_v.at[B]),
        (saved_h, s["saved"]), (wgu_h, wgu), (wd_h, wd),
    )
    loads = [pltpu.make_async_copy(a, b, s["load_sem"].at[i]) for i, (a, b) in enumerate(moves)]
    for load in loads:
        load.start()

    barrier = pltpu.get_barrier_semaphore()
    peers = [ring_id((g + d) % ZN) for d in range(1, ZN)]
    peers += [x_id((x + d) % XN) for d in range(1, XN)]
    peers += list(ends)
    for peer in peers:
        pl.semaphore_signal(barrier, inc=1, device_id=peer, device_id_type=MESH)

    for load in loads[:6]:
        load.wait()
    routing = {}
    for t in (B, F):
        route = r_v[t]
        ranks, counts = route_ranks(route)
        match = choice_match(route, ranks, 48)
        pick = jnp.where(match[0] | match[1], 1.0, 0.0).astype(jnp.bfloat16)
        name = lax.broadcasted_iota(jnp.int32, (8, 1), 0)
        mine = jnp.sum(jnp.where(name == expert, counts, 0.0), axis=0, keepdims=True)
        routing[t] = (route, ranks, mine > BASE + 0.5)
        upper = lax.broadcasted_iota(jnp.int32, (16, 256), 0) < 8
        for b in range(8):
            rows = dot(pick, xin[t, :, b * 512 : (b + 1) * 512])
            over = jnp.where(upper, rows[32:48, :256], rows[32:48, 256:]).astype(jnp.bfloat16)
            for hi in range(2):
                s["zsendn"][t, hi * 8 + b] = rows[hi * 16 : hi * 16 + 16].astype(jnp.bfloat16)
                s["zsendo"][t, hi * 8 + b] = over

    def busiest_only(t, value):
        return jnp.where(routing[t][2], value, 0.0)

    pl.semaphore_wait(barrier, len(peers))

    def rows_to_ring(st):
        t, kind = st
        for d in Z_ORDER:
            z_copy(st, d).start()
        s["zrecv" + kind][t, g] = s["zsend" + kind][t, g]

    rows_to_ring(STREAMS[0])
    for copy in wx:
        copy.start()
    rows_to_ring(STREAMS[1])

    s["c_no"][...] = norm_out()
    s["c_nb"][...] = norm_back()
    for half in range(2):
        s["c_oo"][half] = over_out(half)
        s["c_ob"][half] = over_back(half)
    loads[6].wait()
    for i in range(XN):
        found = dot(stash_rows(chunk_of(i)), s["saved"][...])
        s["kept_n"][i // 2, (i % 2) * NORM : (i % 2 + 1) * NORM] = found[:NORM]
        late = busiest_only(B, found[NORM:])
        if i == 0:
            s["kept_o"][0] = late
        else:
            s["sv_s"][i] = late.astype(jnp.bfloat16)
            sv_copy(i).start()

    def rows_to_x(st):
        t, kind = st
        for d in range(1, ZN):
            z_copy(st, d).wait_recv()
        got = s["zrecv" + kind][t].reshape(256, WIDTH[kind])
        if kind == "n":
            moved = dot(s["c_no"][...], got).astype(jnp.bfloat16)
        else:
            moved = jnp.concatenate([dot(s["c_oo"][0], got), dot(s["c_oo"][1], got)], axis=1).astype(jnp.bfloat16)
        for xx in range(XN):
            s["xsend" + kind][t, xx] = moved[xx * NORM : (xx + 1) * NORM] if kind == "n" else moved
        for d in (2, 1, 3):
            x_copy(st, d).start()
        s["xrecv" + kind][t, x] = s["xsend" + kind][t, x]
        c_copy(st, 0).start()

    def rows_to_sibling(st):
        for i in (1, 3, 2):
            x_copy(st, i).wait_recv()
            c_copy(st, i).start()

    rows_to_ring(STREAMS[2])
    rows_to_ring(STREAMS[3])

    for load in loads[7:]:
        load.wait()
    for copy in wx:
        copy.wait_recv()
    for k, shift in enumerate(SHIFTS):
        dest = (zl + shift) % LINE
        at = k * 128
        s["up_b"][0, :, at : at + 128] = jnp.transpose(wd[dest, core])
        s["up_b"][1, :, at : at + 128] = jnp.transpose(wd_s[dest])
        for a in range(2):
            at = k * 256 + a * 128
            s["up_f"][0, :, at : at + 128] = jnp.transpose(wgu[a, dest, core])
            s["up_f"][1, :, at : at + 128] = jnp.transpose(wgu_s[a, dest])

    def products(st):
        t, kind = st
        up = s["up_f"] if t == F else s["up_b"]
        units = 256 if t == F else 128
        for i in range(XN):
            c_copy(st, i).wait_recv()
        ats = [chunk_of(i) for i in range(XN)]
        mine = jnp.concatenate([s["xrecv" + kind][t, at] for at in ats], axis=0)
        other = jnp.concatenate([s["xsib" + kind][t, at] for at in ats], axis=0)
        for k in range(4):
            lanes = slice(k * units, (k + 1) * units)
            part = dot(mine, up[0, :, lanes]) + dot(other, up[1, :, lanes])
            if kind == "o":
                part = busiest_only(t, part)
                s[f"xr_own{t}"][k] = part[:LATE]
                for i in range(1, XN):
                    s[f"xr_s{t}"][i, k] = part[i * LATE : (i + 1) * LATE].astype(jnp.bfloat16)
                continue
            for q in range(2):
                rows = part[q * 2 * NORM : (q + 1) * 2 * NORM]
                if k == 3:
                    piece("own", st, q)[...] = rows
                else:
                    piece("rs_s", st, q)[k] = rows.astype(jnp.bfloat16)
                    rs_copy(st, q, k).start()
        if kind == "o":
            for i in (2, 1, 3):
                xr_copy(t, i).start()

    def spread_sum(st):
        t = st[0]
        for i in range(1, XN):
            xr_copy(t, i).wait_recv()
        for k in range(4):
            total = s[f"xr_own{t}"][k]
            for i in range(1, XN):
                total = total + s[f"xr_r{t}"][i, k].astype(jnp.float32)
            if k == 3:
                piece("own", st, 0)[...] = total
            else:
                piece("rs_s", st, 0)[k] = total.astype(jnp.bfloat16)
                rs_copy(st, 0, k).start()

    def activate(st):
        for q in range(PIECES[st[1]]):
            total = piece("own", st, q)[...]
            for k in range(3):
                rs_copy(st, q, k).wait_recv()
                total = total + piece("rs_r", st, q)[k].astype(jnp.float32)
            hid = units_of(st, q)
            if st[0] == F:
                gate, up = total[:, :128], total[:, 128:]
                hid[core, 0, :, block_at(zl)] = (gate * sigmoid(gate) * up).astype(jnp.bfloat16)
            else:
                stash = s["kept_" + st[1]][q]
                gate, up = stash[:, :128], stash[:, 128:]
                sig = sigmoid(gate)
                slope = sig * (1.0 + gate * (1.0 - sig))
                hid[core, 0, :, block_at(zl)] = (total * up * slope).astype(jnp.bfloat16)
                hid[core, 1, :, block_at(zl)] = (total * (gate * sig)).astype(jnp.bfloat16)
            for k in range(3):
                ag_copy(st, q, k).start()

    def units_to_sibling(st):
        for q in range(PIECES[st[1]]):
            for k in range(3):
                ag_copy(st, q, k).wait_recv()
            as_copy(st, q).start()
        if st[1] == "o":
            for i in (2, 1, 3):
                xg_copy(st[0], i).start()

    def spread_units(st):
        for i in (1, 3, 2):
            xg_copy(st[0], i).wait_recv()
            xa_copy(st[0], i).start()

    def down(t, hid):
        def rows(c, a):
            return jnp.concatenate([one[c, a] for one in hid], axis=0)

        if t == F:
            return dot(rows(0, 0), wd[:, 0].reshape(512, 512)) + dot(rows(1, 0), wd[:, 1].reshape(512, 512))
        total = None
        for c in range(2):
            for a in range(2):
                part = dot(rows(c, a), wgu[a, :, c].reshape(512, 512))
                total = part if total is None else total + part
        return total

    def back_to_x(st):
        t, kind = st
        rows = KINDS[kind]
        if kind == "o":
            as_copy(st, 0).wait_recv()
            for i in range(1, XN):
                xa_copy(t, i).wait_recv()
            hid = [s[f"hid{t}o"].at[chunk_of(i)] for i in range(XN)]
            made = busiest_only(t, down(t, hid)).astype(jnp.bfloat16)
            for i in range(XN):
                part = made[i * rows : (i + 1) * rows]
                if i == 0:
                    s["orecvo"][t, x] = part
                else:
                    s["oreto"][t, chunk_of(i)] = part
                    b_copy(st, i).start()
            return
        for q in (1, 0):
            as_copy(st, q).wait_recv()
            made = down(t, [piece("hid", st, q)]).astype(jnp.bfloat16)
            for i in (2 * q, 2 * q + 1):
                part = made[(i % 2) * rows : (i % 2 + 1) * rows]
                if i == 0:
                    s["orecv" + kind][t, x] = part
                else:
                    s["oret" + kind][t, chunk_of(i)] = part
                    b_copy(st, i).start()

    def rows_to_sources(st):
        t, kind = st
        for i in range(1, XN):
            b_copy(st, i).wait_recv()
        got = s["orecv" + kind][t].reshape(XN * KINDS[kind], 512)
        if kind == "n":
            moved = dot(s["c_nb"][...], got)
        else:
            moved = dot(s["c_ob"][0], got[:, :256]) + dot(s["c_ob"][1], got[:, 256:])
        s["wsend" + kind][t] = moved.astype(jnp.bfloat16).reshape(ZN, 16, WIDTH[kind])
        for d in range(1, ZN):
            w_copy(st, d).start()
        s["wrecv" + kind][t, g] = s["wsend" + kind][t, g]

    begun = set()

    def combine(st):
        t, kind = st
        route, ranks, _ = routing[t]
        for d in range(1, ZN):
            w_copy(st, d).wait_recv()
        got = s["wrecv" + kind]
        for half in range(2):
            parts = gate_parts(route, g_v[t], ranks, half)
            parts = parts[:, 0:32] if kind == "n" else parts[:, 32:64]
            for b in range(8):
                rows = jnp.concatenate([got[t, b], got[t, 8 + b]], axis=0)
                if kind == "n":
                    rows = rows[:, half * 256 : (half + 1) * 256]
                mixed = dot(parts, rows)
                mixed = mixed[0:16] + mixed[16:32] + mixed[32:48]
                at = pl.ds(b * 512 + half * 256, 256)
                if t in begun:
                    comb[t, :, at] = (mix[t, :, at] + mixed).astype(jnp.bfloat16)
                else:
                    mix[t, :, at] = mixed
        if t in begun:
            y_copy(t).start()
        begun.add(t)

    def late_stash(st):
        if st[0] == B:
            for i in range(1, XN):
                sv_copy(i).wait_recv()
                s["kept_o"][0] += s["sv_r"][i].astype(jnp.float32)
        spread_sum(st)

    first = [rows_to_x, rows_to_sibling, products]
    last = [back_to_x, rows_to_sources, combine]
    steps = {
        "n": first + [activate, units_to_sibling] + last,
        "o": first + [late_stash, activate, units_to_sibling, spread_units] + last,
    }
    for turn in range(len(steps["o"]) + max(LAG)):
        for st, lag in zip(STREAMS, LAG):
            if 0 <= turn - lag < len(steps[st[1]]):
                steps[st[1]][turn - lag](st)

    for copy in wx:
        copy.wait_send()
    for st in STREAMS:
        for d in range(1, ZN):
            z_copy(st, d).wait_send()
            w_copy(st, d).wait_send()
        for i in range(XN):
            c_copy(st, i).wait_send()
        for i in range(1, XN):
            x_copy(st, i).wait_send()
            b_copy(st, i).wait_send()
        for q in range(PIECES[st[1]]):
            as_copy(st, q).wait_send()
            for k in range(3):
                rs_copy(st, q, k).wait_send()
                ag_copy(st, q, k).wait_send()
    for i in range(1, XN):
        sv_copy(i).wait_send()
        for t in (B, F):
            for copy in (xr_copy, xg_copy, xa_copy):
                copy(t, i).wait_send()
    for t in (B, F):
        y_copy(t).wait()


def on_device(x_f, r_f, g_f, x_b, r_b, g_b, gate_up, down, saved):
    in_hbm = pl.BlockSpec(memory_space=pltpu.HBM)
    out = jax.ShapeDtypeStruct((16, 4096), jnp.bfloat16)
    call = pl.pallas_call(
        kernel,
        out_shape=[out, out],
        in_specs=[in_hbm] * 9,
        out_specs=[in_hbm, in_hbm],
        scratch_shapes=list(buffers().values()),
        compiler_params=pltpu.CompilerParams(
            collective_id=0, has_side_effects=True, vmem_limit_bytes=60 * 1024 * 1024
        ),
        cost_estimate=pl.CostEstimate(flops=4 * 10**9, bytes_accessed=8 * 10**6, transcendentals=10**6),
    )
    next_input, prior_gradient = call(
        x_f[0], r_f[0].T, g_f[0].T, x_b[0], r_b[0].T, g_b[0].T,
        gate_up.reshape(2, 4, 2, 128, 512), down.reshape(4, 2, 128, 512), saved[0, 0],
    )
    return next_input[None], prior_gradient[None]


def solution(mesh):
    row = P("pipe", "expert", None)
    wide = P("pipe", "expert", None, None)
    return jax.shard_map(
        on_device,
        mesh=mesh,
        in_specs=(row,) * 6 + (wide,) * 3,
        out_specs=(row, row),
        check_vma=False,
    )
```

```python
import jax
import jax.numpy as jnp
from jax import lax
from jax.experimental import pallas as pl
from jax.experimental.pallas import tpu as pltpu
from jax.sharding import PartitionSpec as P

GROUP = 8
BASE = 4
OVER = 5
ZN = 16
XN = 4
LINE = 4
NORM = ZN * BASE
LATE = ZN * OVER
CHUNK = NORM + LATE
F, B = 0, 1
KINDS = {"n": NORM, "o": LATE}
WIDTH = {"n": 512, "o": 256}
STREAMS = ((B, "o"), (B, "n"), (F, "o"), (F, "n"))
Z_ORDER = (8, 7, 9, 6, 10, 5, 11, 4, 12, 3, 13, 2, 14, 1, 15)
W_ORDER = Z_ORDER + (0,)
ORDER = (
    0, 10, 1, 2, 11, 30, 12, 20, 3, 31,
    13, 32, 4, 21, 22, 14, 33, 23, 5, 15,
    34, 24, 16, 35, 17, 25, 36, 6, 37, 18,
    7, 26, 27, 38, 8, 28, 39, 19, 9, 29,
)
PIECES = {"n": 2, "o": 1}
MESH = pl.DeviceIdType.MESH


def one_hot(target, width):
    col = lax.broadcasted_iota(jnp.int32, (target.shape[0], width), 1)
    return jnp.where(col == target, 1.0, 0.0).astype(jnp.bfloat16)


def fifth(v):
    return (v * 205) >> 10


def rows_of(count):
    return lax.broadcasted_iota(jnp.int32, (count, 1), 0)


def norm_out():
    r = rows_of(256)
    return one_hot(((r >> 2) & 15) * 16 + (r >> 6) * 4 + (r & 3), 256)


def norm_back():
    r = rows_of(256)
    return one_hot(((r >> 2) & 3) * 64 + (r >> 4) * 4 + (r & 3), 256)


def over_out(half):
    r = rows_of(80)
    g = fifth(r)
    return one_hot(g * 16 + half * 8 + r - 5 * g, 256)


def over_back(half):
    r = rows_of(256)
    j = r & 7
    want = jnp.where((((r >> 3) & 1) == half) & (j < OVER), (r >> 4) * 5 + j, -1)
    one = one_hot(want, 80)
    return jnp.concatenate([one] * XN, axis=1)


def stash_rows(x):
    r = rows_of(CHUNK)
    k = r - NORM
    is_norm = k < 0
    g = jnp.where(is_norm, r >> 2, fifth(k))
    slot = jnp.where(is_norm, r & 3, 4 + k - 5 * g)
    return one_hot(((g & 7) * 8 + x * 2 + (g >> 3)) * 9 + slot, XN * CHUNK)


def dot(a, b):
    return jnp.dot(a, b, preferred_element_type=jnp.float32)


def dot_t(a, b):
    return lax.dot_general(a, b, (((1,), (1,)), ((), ())), preferred_element_type=jnp.float32)


def sigmoid(v):
    return 1.0 / (1.0 + jnp.exp(-v))


def route_ranks(route):
    name = lax.broadcasted_iota(jnp.int32, (8, 16), 0)
    picks = [route[k : k + 1] for k in range(2)]
    hits = jnp.where(picks[0] == name, 1.0, 0.0) + jnp.where(picks[1] == name, 1.0, 0.0)
    row = lax.broadcasted_iota(jnp.int32, (16, 16), 0)
    col = lax.broadcasted_iota(jnp.int32, (16, 16), 1)
    earlier = jnp.where(row < col, 1.0, 0.0).astype(jnp.bfloat16)
    before = dot(hits.astype(jnp.bfloat16), earlier)
    ranks = [
        jnp.sum(jnp.where(pick == name, before, 0.0), axis=0, keepdims=True).astype(jnp.int32) for pick in picks
    ]
    return ranks, jnp.sum(hits, axis=1, keepdims=True)


def choice_match(route, ranks, rows, half=None):
    row = lax.broadcasted_iota(jnp.int32, (rows, 16), 0)
    is_norm = row < 32
    expert = ((row >> 2) & 3) * 2 + (row >> 4)
    slot = jnp.where(is_norm, row & 3, 4 + (row & 7))
    if half is not None:
        slot = jnp.where(is_norm | (((row >> 3) & 1) == half), slot, 99)
    return [
        (slot == ranks[k]) & ((expert == route[k : k + 1]) | jnp.logical_not(is_norm)) for k in range(2)
    ]


def gate_parts(route, gates, ranks, half):
    match = choice_match(route, ranks, 64, half)
    total = jnp.where(match[0], gates[0:1], 0.0) + jnp.where(match[1], gates[1:2], 0.0)
    total = jnp.concatenate([total, jnp.zeros((64, 16), jnp.float32)], axis=0)
    total = jnp.concatenate([total, jnp.zeros((128, 112), jnp.float32)], axis=1)
    total = jnp.transpose(total)[:16, :64]
    high = total.astype(jnp.bfloat16)
    rest = total - high.astype(jnp.float32)
    middle = rest.astype(jnp.bfloat16)
    low = (rest - middle.astype(jnp.float32)).astype(jnp.bfloat16)
    return jnp.concatenate([high, middle, low], axis=0)


def buffers():
    bf16, f32 = jnp.bfloat16, jnp.float32
    out = {
        "xin": pltpu.VMEM((2, 16, 4096), bf16),
        "r_v": pltpu.VMEM((2, 2, 16), jnp.int32),
        "rn_v": pltpu.VMEM((2, 2, 16), jnp.int32),
        "gn_v": pltpu.VMEM((2, 2, 16), f32),
        "wgu": pltpu.VMEM((2, 4, 2, 128, 512), bf16),
        "wd": pltpu.VMEM((4, 2, 128, 512), bf16),
        "wgu_s": pltpu.VMEM((2, 4, 128, 512), bf16),
        "wd_s": pltpu.VMEM((4, 128, 512), bf16),
        "up_f": pltpu.VMEM((2, 512, 4 * 256), bf16),
        "up_b": pltpu.VMEM((2, 512, 4 * 128), bf16),
        "saved": pltpu.VMEM((576, 256), bf16),
        "c_no": pltpu.VMEM((256, 256), bf16),
        "c_oo": pltpu.VMEM((2, 80, 256), bf16),
        "c_nb": pltpu.VMEM((256, 256), bf16),
        "c_ob": pltpu.VMEM((2, 256, XN * LATE), bf16),
        "kept_n": pltpu.VMEM((2, 2 * NORM, 256), f32),
        "kept_o": pltpu.VMEM((1, LATE, 256), f32),
        "sv_s": pltpu.VMEM((XN, LATE, 256), bf16),
        "sv_r": pltpu.VMEM((XN, LATE, 256), bf16),
        "mix": pltpu.VMEM((2, 16, 4096), f32),
        "comb": pltpu.VMEM((2, 16, 4096), bf16),
    }
    for kind, rows in KINDS.items():
        for name in ("zsend", "zrecv", "wsend", "wrecv"):
            out[name + kind] = pltpu.VMEM((2, ZN, 16, WIDTH[kind]), bf16)
        for name in ("xsend", "xrecv", "xsib", "oret", "orecv"):
            out[name + kind] = pltpu.VMEM((2, XN, rows, 512), bf16)
    for t in (F, B):
        units = 256 if t == F else 128
        parts = 1 if t == F else 2
        out[f"xr_own{t}"] = pltpu.VMEM((4, LATE, units), f32)
        out[f"xr_s{t}"] = pltpu.VMEM((XN, 4, LATE, units), bf16)
        out[f"xr_r{t}"] = pltpu.VMEM((XN, 4, LATE, units), bf16)
        for kind, rows in (("n", 2 * NORM), ("o", LATE)):
            out[f"own{t}{kind}"] = pltpu.VMEM((PIECES[kind], 2, rows, units), f32)
            for way in "sr":
                if kind == "o":
                    out[f"rs_{way}{t}o"] = pltpu.VMEM((1, 3, rows, units), bf16)
                else:
                    out[f"na_{way}{t}n"] = pltpu.VMEM((2, 2, rows, units), bf16)
                    out[f"fa_{way}{t}n"] = pltpu.VMEM((2, rows, units), bf16)
            count = 2 if kind == "n" else XN
            out[f"hid{t}{kind}"] = pltpu.VMEM((count, 2, parts, rows, 512), bf16)
    dma = pltpu.SemaphoreType.DMA
    out["load_sem"] = dma((7,))
    out["wx_sem"] = dma((2, 2))
    for kind in KINDS:
        for name in ("z", "w"):
            out[name + kind + "_sem"] = dma((2, 2, ZN))
        for name in ("x", "c", "b"):
            out[name + kind + "_sem"] = dma((2, 2, XN))
        out["as" + kind + "_sem"] = dma((2, 2, PIECES[kind]))
        for name in ("rs", "ag"):
            out[name + kind + "_sem"] = dma((2, 2, PIECES[kind], 3))
    for name in ("xr", "xg", "xa"):
        out[name + "_sem"] = dma((2, 2, XN))
    for name in ("na", "fa"):
        out[name + "_sem"] = dma((2, 2, 2))
    out["sv_sem"] = dma((2, XN))
    out["y_sem"] = dma((2, 2, 2))
    out["out_sem"] = dma((2,))
    return out


def kernel(x_f, r_f, g_f, x_b, r_b, g_b, wgu_h, wd_h, saved_h, out_f, out_b, *scratch):
    s = dict(zip(buffers(), scratch))
    xin, r_v = s["xin"], s["r_v"]
    wgu, wd, wgu_s, wd_s = s["wgu"], s["wd"], s["wgu_s"], s["wd_s"]
    comb, mix = s["comb"], s["mix"]

    pipe = lax.axis_index("pipe")
    expert = lax.axis_index("expert")
    y, h = pipe // 8, pipe % 8
    zl, core = h // 2, h % 2
    x, zh = expert // 2, expert % 2
    g = zh * 8 + h
    near, far = zl + 1 - 2 * (zl % 2), (zl + 2) % LINE
    cross = (near + 2) % LINE
    order = (cross, near, far, zl)

    def ring_id(gg, section=y):
        return (section * 8 + gg % 8, x * 2 + gg // 8)

    def x_id(xx):
        return (pipe, xx * 2 + zh)

    def line_id(zz):
        return (y * 8 + zz * 2 + core, expert)

    def chunk_of(i):
        return (x + XN - i) % XN

    sib_id = (pipe + 1 - 2 * core, expert)
    after = ((y + 1) % 8, (y + 7) % 8)

    def remote(src, dst, ss, rs, dev):
        return pltpu.make_async_remote_copy(
            src_ref=src, dst_ref=dst, send_sem=ss, recv_sem=rs, device_id=dev, device_id_type=MESH
        )

    def pair(name, *at):
        sem = s[name + "_sem"]
        return sem.at[(0,) + at], sem.at[(1,) + at]

    def piece(name, st, q):
        return s[f"{name}{st[0]}{st[1]}"].at[q]

    def block_at(zz):
        return pl.ds(pl.multiple_of(zz * 128, 128), 128)

    def z_copy(st, d):
        t, kind = st
        to = (g + d) % ZN
        return remote(s["zsend" + kind].at[t, to], s["zrecv" + kind].at[t, g], *pair("z" + kind, t, d), ring_id(to))

    def x_copy(st, d):
        t, kind = st
        to = (x + d) % XN
        return remote(s["xsend" + kind].at[t, to], s["xrecv" + kind].at[t, x], *pair("x" + kind, t, d), x_id(to))

    def c_copy(st, i):
        t, kind = st
        at = chunk_of(i)
        return remote(s["xrecv" + kind].at[t, at], s["xsib" + kind].at[t, at], *pair("c" + kind, t, i), sib_id)

    def units_of(st, q):
        return piece("hid", st, q if st[1] == "n" else x)

    def sv_copy(i):
        return remote(s["sv_s"].at[i], s["sv_r"].at[i], *pair("sv", i), x_id(chunk_of(i)))

    def xr_copy(t, i):
        return remote(s[f"xr_s{t}"].at[i], s[f"xr_r{t}"].at[i], *pair("xr", t, i), x_id(chunk_of(i)))

    def rs_copy(st, q, k):
        src, dst = piece("rs_s", st, q).at[k], piece("rs_r", st, q).at[k]
        return remote(src, dst, *pair("rs" + st[1], st[0], q, k), line_id(order[k]))

    def near_copy(st, q):
        src, dst = piece("na_s", st, q), piece("na_r", st, q)
        return remote(src, dst, *pair("na", st[0], q), line_id(near))

    def far_copy(st, q):
        src, dst = piece("fa_s", st, q), piece("fa_r", st, q)
        return remote(src, dst, *pair("fa", st[0], q), line_id(far))

    def ag_copy(st, q, k):
        here = units_of(st, q).at[core, :, :, block_at(zl)]
        return remote(here, here, *pair("ag" + st[1], st[0], q, k), line_id(order[k]))

    def relay_copy(st, q):
        here = units_of(st, q).at[core, :, :, block_at(far)]
        return remote(here, here, *pair("agn", st[0], q, 0), line_id(near))

    def as_copy(st, q):
        here = units_of(st, q).at[core]
        return remote(here, here, *pair("as" + st[1], st[0], q), sib_id)

    def xg_copy(t, i):
        here = s[f"hid{t}o"].at[x, core]
        return remote(here, here, *pair("xg", t, i), x_id((x + i) % XN))

    def xa_copy(t, i):
        here = s[f"hid{t}o"].at[chunk_of(i), core]
        return remote(here, here, *pair("xa", t, i), sib_id)

    def b_copy(st, i):
        t, kind = st
        to = chunk_of(i)
        return remote(s["oret" + kind].at[t, to], s["orecv" + kind].at[t, x], *pair("b" + kind, t, i), x_id(to))

    def w_copy(st, d):
        t, kind = st
        to = (g + d) % ZN
        src, dst = s["wsend" + kind].at[t, to], s["wrecv" + kind].at[t, g]
        return remote(src, dst, *pair("w" + kind, t, d), ring_id(to, after[t]))

    def choices(t):
        dev = ring_id(g, after[t])
        return [
            remote((r_f, r_b)[t], s["rn_v"].at[t], *pair("y", t, 0), dev),
            remote((g_f, g_b)[t], s["gn_v"].at[t], *pair("y", t, 1), dev),
        ]

    def out_copy(t):
        return pltpu.make_async_copy(comb.at[t], (out_f, out_b)[t], s["out_sem"].at[t])

    wx = [
        remote(wgu_h.at[:, :, 1 - core], wgu_s, *pair("wx", 0), sib_id),
        remote(wd_h.at[:, 1 - core], wd_s, *pair("wx", 1), sib_id),
    ]

    moves = (
        (r_b, r_v.at[B]), (x_b, xin.at[B]), (r_f, r_v.at[F]), (x_f, xin.at[F]),
        (saved_h, s["saved"]), (wgu_h, wgu), (wd_h, wd),
    )
    loads = [pltpu.make_async_copy(a, b, s["load_sem"].at[i]) for i, (a, b) in enumerate(moves)]
    for load in loads:
        load.start()

    barrier = pltpu.get_barrier_semaphore()
    peers = [ring_id((g + d) % ZN) for d in range(1, ZN)]
    peers += [x_id((x + d) % XN) for d in range(1, XN)]
    peers += [ring_id(gg, section) for section in after for gg in range(ZN)]
    for peer in peers:
        pl.semaphore_signal(barrier, inc=1, device_id=peer, device_id_type=MESH)

    for load in loads[:4]:
        load.wait()
    routing = {}
    for t in (B, F):
        route = r_v[t]
        ranks, counts = route_ranks(route)
        match = choice_match(route, ranks, 48)
        pick = jnp.where(match[0] | match[1], 1.0, 0.0).astype(jnp.bfloat16)
        name = lax.broadcasted_iota(jnp.int32, (8, 1), 0)
        mine = jnp.sum(jnp.where(name == expert, counts, 0.0), axis=0, keepdims=True)
        routing[t] = mine > BASE + 0.5
        upper = lax.broadcasted_iota(jnp.int32, (16, 256), 0) < 8
        for b in range(8):
            rows = dot(pick, xin[t, :, b * 512 : (b + 1) * 512])
            over = jnp.where(upper, rows[32:48, :256], rows[32:48, 256:]).astype(jnp.bfloat16)
            for hi in range(2):
                s["zsendn"][t, hi * 8 + b] = rows[hi * 16 : hi * 16 + 16].astype(jnp.bfloat16)
                s["zsendo"][t, hi * 8 + b] = over

    def busiest_only(t, value):
        return jnp.where(routing[t], value, 0.0)

    pl.semaphore_wait(barrier, len(peers))

    def rows_to_ring(st):
        t, kind = st
        for d in Z_ORDER:
            z_copy(st, d).start()
        s["zrecv" + kind][t, g] = s["zsend" + kind][t, g]

    rows_to_ring(STREAMS[0])
    for copy in wx:
        copy.start()
    rows_to_ring(STREAMS[1])
    for t in (B, F):
        for copy in choices(t):
            copy.start()

    s["c_no"][...] = norm_out()
    s["c_nb"][...] = norm_back()
    for half in range(2):
        s["c_oo"][half] = over_out(half)
        s["c_ob"][half] = over_back(half)
    loads[4].wait()
    for i in range(XN):
        found = dot(stash_rows(chunk_of(i)), s["saved"][...])
        s["kept_n"][i // 2, (i % 2) * NORM : (i % 2 + 1) * NORM] = found[:NORM]
        late = busiest_only(B, found[NORM:])
        if i == 0:
            s["kept_o"][0] = late
        else:
            s["sv_s"][i] = late.astype(jnp.bfloat16)
            sv_copy(i).start()

    def rows_to_x(st):
        t, kind = st
        for d in range(1, ZN):
            z_copy(st, d).wait_recv()
        got = s["zrecv" + kind][t].reshape(256, WIDTH[kind])
        if kind == "n":
            moved = dot(s["c_no"][...], got).astype(jnp.bfloat16)
        else:
            moved = jnp.concatenate([dot(s["c_oo"][0], got), dot(s["c_oo"][1], got)], axis=1).astype(jnp.bfloat16)
        for xx in range(XN):
            s["xsend" + kind][t, xx] = moved[xx * NORM : (xx + 1) * NORM] if kind == "n" else moved
        for d in (2, 1, 3):
            x_copy(st, d).start()
        s["xrecv" + kind][t, x] = s["xsend" + kind][t, x]
        c_copy(st, 0).start()

    def rows_to_sibling(st):
        for i in (1, 3, 2):
            x_copy(st, i).wait_recv()
            c_copy(st, i).start()

    rows_to_ring(STREAMS[2])
    rows_to_ring(STREAMS[3])

    def turn_weights():
        for load in loads[5:]:
            load.wait()
        for copy in wx:
            copy.wait_recv()
        for k, dest in enumerate(order):
            at = k * 128
            s["up_b"][0, :, at : at + 128] = jnp.transpose(wd[dest, core])
            s["up_b"][1, :, at : at + 128] = jnp.transpose(wd_s[dest])
            for a in range(2):
                at = k * 256 + a * 128
                s["up_f"][0, :, at : at + 128] = jnp.transpose(wgu[a, dest, core])
                s["up_f"][1, :, at : at + 128] = jnp.transpose(wgu_s[a, dest])

    def products(st):
        t, kind = st
        up = s["up_f"] if t == F else s["up_b"]
        units = 256 if t == F else 128
        for i in range(XN):
            c_copy(st, i).wait_recv()
        ats = [chunk_of(i) for i in range(XN)]
        mine = jnp.concatenate([s["xrecv" + kind][t, at] for at in ats], axis=0)
        other = jnp.concatenate([s["xsib" + kind][t, at] for at in ats], axis=0)
        for k in range(4):
            lanes = slice(k * units, (k + 1) * units)
            part = dot(mine, up[0, :, lanes]) + dot(other, up[1, :, lanes])
            if kind == "o":
                part = busiest_only(t, part)
                s[f"xr_own{t}"][k] = part[:LATE]
                for i in range(1, XN):
                    s[f"xr_s{t}"][i, k] = part[i * LATE : (i + 1) * LATE].astype(jnp.bfloat16)
                continue
            for q in range(2):
                rows = part[q * 2 * NORM : (q + 1) * 2 * NORM]
                if k < 2:
                    piece("na_s", st, q)[k] = rows.astype(jnp.bfloat16)
                    if k == 1:
                        near_copy(st, q).start()
                else:
                    piece("own", st, q)[k - 2] = rows
        if kind == "o":
            for i in (2, 1, 3):
                xr_copy(t, i).start()

    def spread_sum(st):
        t = st[0]
        for i in range(1, XN):
            xr_copy(t, i).wait_recv()
        for k in range(4):
            total = s[f"xr_own{t}"][k]
            for i in range(1, XN):
                total = total + s[f"xr_r{t}"][i, k].astype(jnp.float32)
            if k == 3:
                piece("own", st, 0)[1] = total
            else:
                piece("rs_s", st, 0)[k] = total.astype(jnp.bfloat16)
                rs_copy(st, 0, k).start()

    def pass_on(st):
        for q in range(2):
            near_copy(st, q).wait_recv()
            total = piece("own", st, q)[0] + piece("na_r", st, q)[0].astype(jnp.float32)
            piece("fa_s", st, q)[...] = total.astype(jnp.bfloat16)
            far_copy(st, q).start()

    def activate(st):
        for q in range(PIECES[st[1]]):
            total = piece("own", st, q)[1]
            if st[1] == "n":
                far_copy(st, q).wait_recv()
                total = total + piece("na_r", st, q)[1].astype(jnp.float32)
                total = total + piece("fa_r", st, q)[...].astype(jnp.float32)
            else:
                for k in range(3):
                    rs_copy(st, q, k).wait_recv()
                    total = total + piece("rs_r", st, q)[k].astype(jnp.float32)
            hid = units_of(st, q)
            if st[0] == F:
                gate, up = total[:, :128], total[:, 128:]
                hid[core, 0, :, block_at(zl)] = (gate * sigmoid(gate) * up).astype(jnp.bfloat16)
            else:
                stash = s["kept_" + st[1]][q]
                gate, up = stash[:, :128], stash[:, 128:]
                sig = sigmoid(gate)
                slope = sig * (1.0 + gate * (1.0 - sig))
                hid[core, 0, :, block_at(zl)] = (total * up * slope).astype(jnp.bfloat16)
                hid[core, 1, :, block_at(zl)] = (total * (gate * sig)).astype(jnp.bfloat16)
            for k in (2, 1) if st[1] == "n" else (2, 1, 0):
                ag_copy(st, q, k).start()

    def relay(st):
        for q in range(2):
            ag_copy(st, q, 2).wait_recv()
            relay_copy(st, q).start()

    def units_to_sibling(st):
        for q in range(PIECES[st[1]]):
            ag_copy(st, q, 1).wait_recv()
            if st[1] == "n":
                relay_copy(st, q).wait_recv()
            else:
                ag_copy(st, q, 2).wait_recv()
                ag_copy(st, q, 0).wait_recv()
            as_copy(st, q).start()
        if st[1] == "o":
            for i in (2, 1, 3):
                xg_copy(st[0], i).start()

    def spread_units(st):
        for i in (1, 3, 2):
            xg_copy(st[0], i).wait_recv()
            xa_copy(st[0], i).start()

    def down(t, hid):
        def rows(c, a):
            return jnp.concatenate([one[c, a] for one in hid], axis=0)

        if t == F:
            return dot(rows(0, 0), wd[:, 0].reshape(512, 512)) + dot(rows(1, 0), wd[:, 1].reshape(512, 512))
        total = None
        for c in range(2):
            for a in range(2):
                part = dot(rows(c, a), wgu[a, :, c].reshape(512, 512))
                total = part if total is None else total + part
        return total

    def back_to_x(st):
        t, kind = st
        rows = KINDS[kind]
        if kind == "o":
            as_copy(st, 0).wait_recv()
            for i in range(1, XN):
                xa_copy(t, i).wait_recv()
            hid = [s[f"hid{t}o"].at[chunk_of(i)] for i in range(XN)]
            made = busiest_only(t, down(t, hid)).astype(jnp.bfloat16)
            for i in range(XN):
                part = made[i * rows : (i + 1) * rows]
                if i == 0:
                    s["orecvo"][t, x] = part
                else:
                    s["oreto"][t, chunk_of(i)] = part
                    b_copy(st, i).start()
            return
        for q in (1, 0):
            as_copy(st, q).wait_recv()
            made = down(t, [piece("hid", st, q)]).astype(jnp.bfloat16)
            for i in (2 * q, 2 * q + 1):
                part = made[(i % 2) * rows : (i % 2 + 1) * rows]
                if i == 0:
                    s["orecv" + kind][t, x] = part
                else:
                    s["oret" + kind][t, chunk_of(i)] = part
                    b_copy(st, i).start()

    def rows_to_sources(st):
        t, kind = st
        for i in range(1, XN):
            b_copy(st, i).wait_recv()
        got = s["orecv" + kind][t].reshape(XN * KINDS[kind], 512)
        if kind == "n":
            moved = dot(s["c_nb"][...], got)
        else:
            moved = dot(s["c_ob"][0], got[:, :256]) + dot(s["c_ob"][1], got[:, 256:])
        s["wsend" + kind][t] = moved.astype(jnp.bfloat16).reshape(ZN, 16, WIDTH[kind])
        for d in W_ORDER:
            w_copy(st, d).start()

    begun = set()

    def combine(st):
        t, kind = st
        if t not in begun:
            for copy in choices(t):
                copy.wait_recv()
        route = s["rn_v"][t]
        ranks, _ = route_ranks(route)
        for d in W_ORDER:
            w_copy(st, d).wait_recv()
        got = s["wrecv" + kind]
        for half in range(2):
            parts = gate_parts(route, s["gn_v"][t], ranks, half)
            parts = parts[:, 0:32] if kind == "n" else parts[:, 32:64]
            for b in range(8):
                rows = jnp.concatenate([got[t, b], got[t, 8 + b]], axis=0)
                if kind == "n":
                    rows = rows[:, half * 256 : (half + 1) * 256]
                mixed = dot(parts, rows)
                mixed = mixed[0:16] + mixed[16:32] + mixed[32:48]
                at = pl.ds(b * 512 + half * 256, 256)
                if t in begun:
                    comb[t, :, at] = (mix[t, :, at] + mixed).astype(jnp.bfloat16)
                else:
                    mix[t, :, at] = mixed
        if t in begun:
            out_copy(t).start()
        begun.add(t)

    def late_stash(st):
        if st[0] == B:
            for i in range(1, XN):
                sv_copy(i).wait_recv()
                s["kept_o"][0] += s["sv_r"][i].astype(jnp.float32)
        spread_sum(st)

    first = [rows_to_x, rows_to_sibling, products]
    last = [back_to_x, rows_to_sources, combine]
    steps = {
        "n": first + [pass_on, activate, relay, units_to_sibling] + last,
        "o": first + [late_stash, activate, units_to_sibling, spread_units] + last,
    }
    turned = False
    for at in ORDER:
        st = STREAMS[at // 10]
        steps[st[1]][at % 10](st)
        if at % 10 == 1 and not turned:
            turn_weights()
            turned = True

    for copy in wx:
        copy.wait_send()
    for st in STREAMS:
        for d in range(1, ZN):
            z_copy(st, d).wait_send()
        for d in W_ORDER:
            w_copy(st, d).wait_send()
        for i in range(XN):
            c_copy(st, i).wait_send()
        for i in range(1, XN):
            x_copy(st, i).wait_send()
            b_copy(st, i).wait_send()
        for q in range(PIECES[st[1]]):
            as_copy(st, q).wait_send()
            ag_copy(st, q, 1).wait_send()
            ag_copy(st, q, 2).wait_send()
            if st[1] == "n":
                near_copy(st, q).wait_send()
                far_copy(st, q).wait_send()
                relay_copy(st, q).wait_send()
            else:
                ag_copy(st, q, 0).wait_send()
                for k in range(3):
                    rs_copy(st, q, k).wait_send()
    for i in range(1, XN):
        sv_copy(i).wait_send()
        for t in (B, F):
            for copy in (xr_copy, xg_copy, xa_copy):
                copy(t, i).wait_send()
    for t in (B, F):
        for copy in choices(t):
            copy.wait_send()
        out_copy(t).wait()


def on_device(x_f, r_f, g_f, x_b, r_b, g_b, gate_up, down, saved):
    in_hbm = pl.BlockSpec(memory_space=pltpu.HBM)
    out = jax.ShapeDtypeStruct((16, 4096), jnp.bfloat16)
    call = pl.pallas_call(
        kernel,
        out_shape=[out, out],
        in_specs=[in_hbm] * 9,
        out_specs=[in_hbm, in_hbm],
        scratch_shapes=list(buffers().values()),
        compiler_params=pltpu.CompilerParams(
            collective_id=0, has_side_effects=True, vmem_limit_bytes=60 * 1024 * 1024
        ),
        cost_estimate=pl.CostEstimate(flops=4 * 10**9, bytes_accessed=8 * 10**6, transcendentals=10**6),
    )
    next_input, prior_gradient = call(
        x_f[0], r_f[0].T, g_f[0].T, x_b[0], r_b[0].T, g_b[0].T,
        gate_up.reshape(2, 4, 2, 128, 512), down.reshape(4, 2, 128, 512), saved[0, 0],
    )
    return next_input[None], prior_gradient[None]


def solution(mesh):
    row = P("pipe", "expert", None)
    wide = P("pipe", "expert", None, None)
    return jax.shard_map(
        on_device,
        mesh=mesh,
        in_specs=(row,) * 6 + (wide,) * 3,
        out_specs=(row, row),
        check_vma=False,
    )
```

```python
import jax
import jax.numpy as jnp
from jax import lax
from jax.experimental import pallas as pl
from jax.experimental.pallas import tpu as pltpu
from jax.sharding import PartitionSpec as P

GROUP = 8
BASE = 4
OVER = 5
ZN = 16
XN = 4
LINE = 4
NORM = ZN * BASE
LATE = ZN * OVER
CHUNK = NORM + LATE
F, B = 0, 1
KINDS = {"n": NORM, "o": LATE}
WIDTH = {"n": 512, "o": 256}
STREAMS = ((B, "o"), (B, "n"), (F, "o"), (F, "n"))
Z_ORDER = (8, 7, 9, 6, 10, 5, 11, 4, 12, 3, 13, 2, 14, 1, 15)
W_ORDER = Z_ORDER + (0,)
ENTRY = (3, 0, 1, 2)
ORDER = (
    30, 0, 31, 10, 32, 20, 1, 2, 11, 33,
    21, 12, 22, 3, 34, 13, 4, 35, 23, 36,
    14, 5, 24, 37, 15, 6, 25, 7, 16, 38,
    17, 26, 27, 8, 18, 28, 19, 39, 9, 29,
)
PIECES = {"n": 2, "o": 1}
MESH = pl.DeviceIdType.MESH


def one_hot(target, width):
    col = lax.broadcasted_iota(jnp.int32, (target.shape[0], width), 1)
    return jnp.where(col == target, 1.0, 0.0).astype(jnp.bfloat16)


def fifth(v):
    return (v * 205) >> 10


def rows_of(count):
    return lax.broadcasted_iota(jnp.int32, (count, 1), 0)


def norm_out():
    r = rows_of(256)
    return one_hot(((r >> 2) & 15) * 16 + (r >> 6) * 4 + (r & 3), 256)


def norm_back():
    r = rows_of(256)
    return one_hot(((r >> 2) & 3) * 64 + (r >> 4) * 4 + (r & 3), 256)


def over_out(half):
    r = rows_of(80)
    g = fifth(r)
    return one_hot(g * 16 + half * 8 + r - 5 * g, 256)


def over_back(half):
    r = rows_of(256)
    j = r & 7
    want = jnp.where((((r >> 3) & 1) == half) & (j < OVER), (r >> 4) * 5 + j, -1)
    one = one_hot(want, 80)
    return jnp.concatenate([one] * XN, axis=1)


def stash_rows(x):
    r = rows_of(CHUNK)
    k = r - NORM
    is_norm = k < 0
    g = jnp.where(is_norm, r >> 2, fifth(k))
    slot = jnp.where(is_norm, r & 3, 4 + k - 5 * g)
    return one_hot(((g & 7) * 8 + x * 2 + (g >> 3)) * 9 + slot, XN * CHUNK)


def dot(a, b):
    return jnp.dot(a, b, preferred_element_type=jnp.float32)


def dot_t(a, b):
    return lax.dot_general(a, b, (((1,), (1,)), ((), ())), preferred_element_type=jnp.float32)


def sigmoid(v):
    return 1.0 / (1.0 + jnp.exp(-v))


def route_ranks(route):
    name = lax.broadcasted_iota(jnp.int32, (8, 16), 0)
    picks = [route[k : k + 1] for k in range(2)]
    hits = jnp.where(picks[0] == name, 1.0, 0.0) + jnp.where(picks[1] == name, 1.0, 0.0)
    row = lax.broadcasted_iota(jnp.int32, (16, 16), 0)
    col = lax.broadcasted_iota(jnp.int32, (16, 16), 1)
    earlier = jnp.where(row < col, 1.0, 0.0).astype(jnp.bfloat16)
    before = dot(hits.astype(jnp.bfloat16), earlier)
    ranks = [
        jnp.sum(jnp.where(pick == name, before, 0.0), axis=0, keepdims=True).astype(jnp.int32) for pick in picks
    ]
    return ranks, jnp.sum(hits, axis=1, keepdims=True)


def choice_match(route, ranks, rows, half=None):
    row = lax.broadcasted_iota(jnp.int32, (rows, 16), 0)
    is_norm = row < 32
    expert = ((row >> 2) & 3) * 2 + (row >> 4)
    slot = jnp.where(is_norm, row & 3, 4 + (row & 7))
    if half is not None:
        slot = jnp.where(is_norm | (((row >> 3) & 1) == half), slot, 99)
    return [
        (slot == ranks[k]) & ((expert == route[k : k + 1]) | jnp.logical_not(is_norm)) for k in range(2)
    ]


def gate_parts(route, gates, ranks, half):
    match = choice_match(route, ranks, 64, half)
    total = jnp.where(match[0], gates[0:1], 0.0) + jnp.where(match[1], gates[1:2], 0.0)
    total = jnp.concatenate([total, jnp.zeros((64, 16), jnp.float32)], axis=0)
    total = jnp.concatenate([total, jnp.zeros((128, 112), jnp.float32)], axis=1)
    total = jnp.transpose(total)[:16, :64]
    high = total.astype(jnp.bfloat16)
    rest = total - high.astype(jnp.float32)
    middle = rest.astype(jnp.bfloat16)
    low = (rest - middle.astype(jnp.float32)).astype(jnp.bfloat16)
    return jnp.concatenate([high, middle, low], axis=0)


def buffers():
    bf16, f32 = jnp.bfloat16, jnp.float32
    out = {
        "xin": pltpu.VMEM((2, 16, 4096), bf16),
        "r_v": pltpu.VMEM((2, 2, 16), jnp.int32),
        "rn_v": pltpu.VMEM((2, 2, 16), jnp.int32),
        "gn_v": pltpu.VMEM((2, 2, 16), f32),
        "wgu": pltpu.VMEM((2, 4, 2, 128, 512), bf16),
        "wd": pltpu.VMEM((4, 2, 128, 512), bf16),
        "wgu_s": pltpu.VMEM((2, 4, 128, 512), bf16),
        "wd_s": pltpu.VMEM((4, 128, 512), bf16),
        "up_f": pltpu.VMEM((2, 512, 4 * 256), bf16),
        "up_b": pltpu.VMEM((2, 512, 4 * 128), bf16),
        "saved": pltpu.VMEM((576, 256), bf16),
        "c_no": pltpu.VMEM((256, 256), bf16),
        "c_oo": pltpu.VMEM((2, 80, 256), bf16),
        "c_nb": pltpu.VMEM((256, 256), bf16),
        "c_ob": pltpu.VMEM((2, 256, XN * LATE), bf16),
        "kept_n": pltpu.VMEM((2, 2 * NORM, 256), f32),
        "kept_o": pltpu.VMEM((1, LATE, 256), f32),
        "sv_s": pltpu.VMEM((XN, LATE, 256), bf16),
        "sv_r": pltpu.VMEM((XN, LATE, 256), bf16),
        "mix": pltpu.VMEM((2, 16, 4096), f32),
        "comb": pltpu.VMEM((2, 16, 4096), bf16),
    }
    for kind, rows in KINDS.items():
        for name in ("zsend", "zrecv", "wsend", "wrecv"):
            out[name + kind] = pltpu.VMEM((2, ZN, 16, WIDTH[kind]), bf16)
        for name in ("xsend", "xrecv", "xsib", "oret", "orecv"):
            out[name + kind] = pltpu.VMEM((2, XN, rows, 512), bf16)
    for t in (F, B):
        units = 256 if t == F else 128
        parts = 1 if t == F else 2
        out[f"xr_own{t}"] = pltpu.VMEM((4, LATE, units), f32)
        out[f"xr_s{t}"] = pltpu.VMEM((XN, 4, LATE, units), bf16)
        out[f"xr_r{t}"] = pltpu.VMEM((XN, 4, LATE, units), bf16)
        for kind, rows in (("n", 2 * NORM), ("o", LATE)):
            out[f"own{t}{kind}"] = pltpu.VMEM((PIECES[kind], 2, rows, units), f32)
            for way in "sr":
                if kind == "o":
                    out[f"rs_{way}{t}o"] = pltpu.VMEM((1, 3, rows, units), bf16)
                else:
                    out[f"na_{way}{t}n"] = pltpu.VMEM((2, 2, rows, units), bf16)
                    out[f"fa_{way}{t}n"] = pltpu.VMEM((2, rows, units), bf16)
            count = 2 if kind == "n" else XN
            out[f"hid{t}{kind}"] = pltpu.VMEM((count, 2, parts, rows, 512), bf16)
    dma = pltpu.SemaphoreType.DMA
    out["load_sem"] = dma((7,))
    out["wx_sem"] = dma((2, 2))
    for kind in KINDS:
        for name in ("z", "w"):
            out[name + kind + "_sem"] = dma((2, 2, ZN))
        for name in ("x", "c", "b"):
            out[name + kind + "_sem"] = dma((2, 2, XN))
        out["as" + kind + "_sem"] = dma((2, 2, PIECES[kind]))
        for name in ("rs", "ag"):
            out[name + kind + "_sem"] = dma((2, 2, PIECES[kind], 3))
    for name in ("xr", "xg", "xa"):
        out[name + "_sem"] = dma((2, 2, XN))
    for name in ("na", "fa"):
        out[name + "_sem"] = dma((2, 2, 2))
    out["sv_sem"] = dma((2, XN))
    out["y_sem"] = dma((2, 2, 2))
    out["out_sem"] = dma((2,))
    return out


def kernel(x_f, r_f, g_f, x_b, r_b, g_b, wgu_h, wd_h, saved_h, out_f, out_b, *scratch):
    s = dict(zip(buffers(), scratch))
    xin, r_v = s["xin"], s["r_v"]
    wgu, wd, wgu_s, wd_s = s["wgu"], s["wd"], s["wgu_s"], s["wd_s"]
    comb, mix = s["comb"], s["mix"]

    pipe = lax.axis_index("pipe")
    expert = lax.axis_index("expert")
    y, h = pipe // 8, pipe % 8
    zl, core = h // 2, h % 2
    x, zh = expert // 2, expert % 2
    g = zh * 8 + h
    near, far = zl + 1 - 2 * (zl % 2), (zl + 2) % LINE
    cross = (near + 2) % LINE
    order = (cross, near, far, zl)

    def ring_id(gg, section=y):
        return (section * 8 + gg % 8, x * 2 + gg // 8)

    def x_id(xx):
        return (pipe, xx * 2 + zh)

    def line_id(zz):
        return (y * 8 + zz * 2 + core, expert)

    def chunk_of(i):
        return (x + XN - i) % XN

    sib_id = (pipe + 1 - 2 * core, expert)
    after = ((y + 1) % 8, (y + 7) % 8)

    def remote(src, dst, ss, rs, dev):
        return pltpu.make_async_remote_copy(
            src_ref=src, dst_ref=dst, send_sem=ss, recv_sem=rs, device_id=dev, device_id_type=MESH
        )

    def pair(name, *at):
        sem = s[name + "_sem"]
        return sem.at[(0,) + at], sem.at[(1,) + at]

    def piece(name, st, q):
        return s[f"{name}{st[0]}{st[1]}"].at[q]

    def block_at(zz):
        return pl.ds(pl.multiple_of(zz * 128, 128), 128)

    def z_copy(st, d):
        t, kind = st
        to = (g + d) % ZN
        return remote(s["zsend" + kind].at[t, to], s["zrecv" + kind].at[t, g], *pair("z" + kind, t, d), ring_id(to))

    def x_copy(st, d):
        t, kind = st
        to = (x + d) % XN
        return remote(s["xsend" + kind].at[t, to], s["xrecv" + kind].at[t, x], *pair("x" + kind, t, d), x_id(to))

    def c_copy(st, i):
        t, kind = st
        at = chunk_of(i)
        return remote(s["xrecv" + kind].at[t, at], s["xsib" + kind].at[t, at], *pair("c" + kind, t, i), sib_id)

    def units_of(st, q):
        return piece("hid", st, q if st[1] == "n" else x)

    def sv_copy(i):
        return remote(s["sv_s"].at[i], s["sv_r"].at[i], *pair("sv", i), x_id(chunk_of(i)))

    def xr_copy(t, i):
        return remote(s[f"xr_s{t}"].at[i], s[f"xr_r{t}"].at[i], *pair("xr", t, i), x_id(chunk_of(i)))

    def rs_copy(st, q, k):
        src, dst = piece("rs_s", st, q).at[k], piece("rs_r", st, q).at[k]
        return remote(src, dst, *pair("rs" + st[1], st[0], q, k), line_id(order[k]))

    def near_copy(st, q):
        src, dst = piece("na_s", st, q), piece("na_r", st, q)
        return remote(src, dst, *pair("na", st[0], q), line_id(near))

    def far_copy(st, q):
        src, dst = piece("fa_s", st, q), piece("fa_r", st, q)
        return remote(src, dst, *pair("fa", st[0], q), line_id(far))

    def ag_copy(st, q, k):
        here = units_of(st, q).at[core, :, :, block_at(zl)]
        return remote(here, here, *pair("ag" + st[1], st[0], q, k), line_id(order[k]))

    def relay_copy(st, q):
        here = units_of(st, q).at[core, :, :, block_at(far)]
        return remote(here, here, *pair("agn", st[0], q, 0), line_id(near))

    def as_copy(st, q):
        here = units_of(st, q).at[core]
        return remote(here, here, *pair("as" + st[1], st[0], q), sib_id)

    def xg_copy(t, i):
        here = s[f"hid{t}o"].at[x, core]
        return remote(here, here, *pair("xg", t, i), x_id((x + i) % XN))

    def xa_copy(t, i):
        here = s[f"hid{t}o"].at[chunk_of(i), core]
        return remote(here, here, *pair("xa", t, i), sib_id)

    def b_copy(st, i):
        t, kind = st
        to = chunk_of(i)
        return remote(s["oret" + kind].at[t, to], s["orecv" + kind].at[t, x], *pair("b" + kind, t, i), x_id(to))

    def w_copy(st, d):
        t, kind = st
        to = (g + d) % ZN
        src, dst = s["wsend" + kind].at[t, to], s["wrecv" + kind].at[t, g]
        return remote(src, dst, *pair("w" + kind, t, d), ring_id(to, after[t]))

    def choices(t):
        dev = ring_id(g, after[t])
        return [
            remote((r_f, r_b)[t], s["rn_v"].at[t], *pair("y", t, 0), dev),
            remote((g_f, g_b)[t], s["gn_v"].at[t], *pair("y", t, 1), dev),
        ]

    def out_copy(t):
        return pltpu.make_async_copy(comb.at[t], (out_f, out_b)[t], s["out_sem"].at[t])

    wx = [
        remote(wgu_h.at[:, :, 1 - core], wgu_s, *pair("wx", 0), sib_id),
        remote(wd_h.at[:, 1 - core], wd_s, *pair("wx", 1), sib_id),
    ]

    moves = (
        (r_b, r_v.at[B]), (x_b, xin.at[B]), (r_f, r_v.at[F]), (x_f, xin.at[F]),
        (saved_h, s["saved"]), (wgu_h, wgu), (wd_h, wd),
    )
    loads = [pltpu.make_async_copy(a, b, s["load_sem"].at[i]) for i, (a, b) in enumerate(moves)]
    for load in loads:
        load.start()

    barrier = pltpu.get_barrier_semaphore()
    peers = [ring_id((g + d) % ZN) for d in Z_ORDER]
    peers += [x_id((x + d) % XN) for d in range(1, XN)]
    peers += [ring_id(gg, section) for section in after for gg in range(ZN)]
    for peer in peers:
        pl.semaphore_signal(barrier, inc=1, device_id=peer, device_id_type=MESH)

    for load in loads[:4]:
        load.wait()
    routing = {}
    for t in (B, F):
        route = r_v[t]
        ranks, counts = route_ranks(route)
        match = choice_match(route, ranks, 48)
        pick = jnp.where(match[0] | match[1], 1.0, 0.0).astype(jnp.bfloat16)
        name = lax.broadcasted_iota(jnp.int32, (8, 1), 0)
        mine = jnp.sum(jnp.where(name == expert, counts, 0.0), axis=0, keepdims=True)
        routing[t] = mine > BASE + 0.5
        upper = lax.broadcasted_iota(jnp.int32, (16, 256), 0) < 8
        for b in range(8):
            rows = dot(pick, xin[t, :, b * 512 : (b + 1) * 512])
            over = jnp.where(upper, rows[32:48, :256], rows[32:48, 256:]).astype(jnp.bfloat16)
            for hi in range(2):
                s["zsendn"][t, hi * 8 + b] = rows[hi * 16 : hi * 16 + 16].astype(jnp.bfloat16)
                s["zsendo"][t, hi * 8 + b] = over

    def busiest_only(t, value):
        return jnp.where(routing[t], value, 0.0)

    pl.semaphore_wait(barrier, len(peers))

    def rows_to_ring(st):
        t, kind = st
        for d in Z_ORDER:
            z_copy(st, d).start()
        s["zrecv" + kind][t, g] = s["zsend" + kind][t, g]

    rows_to_ring(STREAMS[ENTRY[0]])
    for copy in wx:
        copy.start()
    rows_to_ring(STREAMS[ENTRY[1]])
    for t in (B, F):
        for copy in choices(t):
            copy.start()

    s["c_no"][...] = norm_out()
    s["c_nb"][...] = norm_back()
    for half in range(2):
        s["c_oo"][half] = over_out(half)
        s["c_ob"][half] = over_back(half)
    loads[4].wait()
    for i in range(XN):
        found = dot(stash_rows(chunk_of(i)), s["saved"][...])
        s["kept_n"][i // 2, (i % 2) * NORM : (i % 2 + 1) * NORM] = found[:NORM]
        late = busiest_only(B, found[NORM:])
        if i == 0:
            s["kept_o"][0] = late
        else:
            s["sv_s"][i] = late.astype(jnp.bfloat16)
            sv_copy(i).start()

    def rows_to_x(st):
        t, kind = st
        for d in range(1, ZN):
            z_copy(st, d).wait_recv()
        got = s["zrecv" + kind][t].reshape(256, WIDTH[kind])
        if kind == "n":
            moved = dot(s["c_no"][...], got).astype(jnp.bfloat16)
        else:
            moved = jnp.concatenate([dot(s["c_oo"][0], got), dot(s["c_oo"][1], got)], axis=1).astype(jnp.bfloat16)
        for xx in range(XN):
            s["xsend" + kind][t, xx] = moved[xx * NORM : (xx + 1) * NORM] if kind == "n" else moved
        for d in (2, 1, 3):
            x_copy(st, d).start()
        s["xrecv" + kind][t, x] = s["xsend" + kind][t, x]
        c_copy(st, 0).start()

    def rows_to_sibling(st):
        for i in (1, 3, 2):
            x_copy(st, i).wait_recv()
            c_copy(st, i).start()

    rows_to_ring(STREAMS[ENTRY[2]])
    rows_to_ring(STREAMS[ENTRY[3]])

    def turn_weights():
        for load in loads[5:]:
            load.wait()
        for copy in wx:
            copy.wait_recv()
        for k, dest in enumerate(order):
            at = k * 128
            s["up_b"][0, :, at : at + 128] = jnp.transpose(wd[dest, core])
            s["up_b"][1, :, at : at + 128] = jnp.transpose(wd_s[dest])
            for a in range(2):
                at = k * 256 + a * 128
                s["up_f"][0, :, at : at + 128] = jnp.transpose(wgu[a, dest, core])
                s["up_f"][1, :, at : at + 128] = jnp.transpose(wgu_s[a, dest])

    def products(st):
        t, kind = st
        up = s["up_f"] if t == F else s["up_b"]
        units = 256 if t == F else 128
        for i in range(XN):
            c_copy(st, i).wait_recv()
        ats = [chunk_of(i) for i in range(XN)]
        mine = jnp.concatenate([s["xrecv" + kind][t, at] for at in ats], axis=0)
        other = jnp.concatenate([s["xsib" + kind][t, at] for at in ats], axis=0)
        for k in range(4):
            lanes = slice(k * units, (k + 1) * units)
            part = dot(mine, up[0, :, lanes]) + dot(other, up[1, :, lanes])
            if kind == "o":
                part = busiest_only(t, part)
                s[f"xr_own{t}"][k] = part[:LATE]
                for i in range(1, XN):
                    s[f"xr_s{t}"][i, k] = part[i * LATE : (i + 1) * LATE].astype(jnp.bfloat16)
                continue
            for q in range(2):
                rows = part[q * 2 * NORM : (q + 1) * 2 * NORM]
                if k < 2:
                    piece("na_s", st, q)[k] = rows.astype(jnp.bfloat16)
                    if k == 1:
                        near_copy(st, q).start()
                else:
                    piece("own", st, q)[k - 2] = rows
        if kind == "o":
            for i in (2, 1, 3):
                xr_copy(t, i).start()

    def spread_sum(st):
        t = st[0]
        for i in range(1, XN):
            xr_copy(t, i).wait_recv()
        for k in range(4):
            total = s[f"xr_own{t}"][k]
            for i in range(1, XN):
                total = total + s[f"xr_r{t}"][i, k].astype(jnp.float32)
            if k == 3:
                piece("own", st, 0)[1] = total
            else:
                piece("rs_s", st, 0)[k] = total.astype(jnp.bfloat16)
                rs_copy(st, 0, k).start()

    def pass_on(st):
        for q in range(2):
            near_copy(st, q).wait_recv()
            total = piece("own", st, q)[0] + piece("na_r", st, q)[0].astype(jnp.float32)
            piece("fa_s", st, q)[...] = total.astype(jnp.bfloat16)
            far_copy(st, q).start()

    def activate(st):
        for q in range(PIECES[st[1]]):
            total = piece("own", st, q)[1]
            if st[1] == "n":
                far_copy(st, q).wait_recv()
                total = total + piece("na_r", st, q)[1].astype(jnp.float32)
                total = total + piece("fa_r", st, q)[...].astype(jnp.float32)
            else:
                for k in range(3):
                    rs_copy(st, q, k).wait_recv()
                    total = total + piece("rs_r", st, q)[k].astype(jnp.float32)
            hid = units_of(st, q)
            if st[0] == F:
                gate, up = total[:, :128], total[:, 128:]
                hid[core, 0, :, block_at(zl)] = (gate * sigmoid(gate) * up).astype(jnp.bfloat16)
            else:
                stash = s["kept_" + st[1]][q]
                gate, up = stash[:, :128], stash[:, 128:]
                sig = sigmoid(gate)
                slope = sig * (1.0 + gate * (1.0 - sig))
                hid[core, 0, :, block_at(zl)] = (total * up * slope).astype(jnp.bfloat16)
                hid[core, 1, :, block_at(zl)] = (total * (gate * sig)).astype(jnp.bfloat16)
            for k in (2, 1) if st[1] == "n" else (2, 1, 0):
                ag_copy(st, q, k).start()

    def relay(st):
        for q in range(2):
            ag_copy(st, q, 2).wait_recv()
            relay_copy(st, q).start()

    def units_to_sibling(st):
        for q in range(PIECES[st[1]]):
            ag_copy(st, q, 1).wait_recv()
            if st[1] == "n":
                relay_copy(st, q).wait_recv()
            else:
                ag_copy(st, q, 2).wait_recv()
                ag_copy(st, q, 0).wait_recv()
            as_copy(st, q).start()
        if st[1] == "o":
            for i in (2, 1, 3):
                xg_copy(st[0], i).start()

    def spread_units(st):
        for i in (1, 3, 2):
            xg_copy(st[0], i).wait_recv()
            xa_copy(st[0], i).start()

    def down(t, hid):
        def rows(c, a):
            return jnp.concatenate([one[c, a] for one in hid], axis=0)

        if t == F:
            return dot(rows(0, 0), wd[:, 0].reshape(512, 512)) + dot(rows(1, 0), wd[:, 1].reshape(512, 512))
        total = None
        for c in range(2):
            for a in range(2):
                part = dot(rows(c, a), wgu[a, :, c].reshape(512, 512))
                total = part if total is None else total + part
        return total

    def back_to_x(st):
        t, kind = st
        rows = KINDS[kind]
        if kind == "o":
            as_copy(st, 0).wait_recv()
            for i in range(1, XN):
                xa_copy(t, i).wait_recv()
            hid = [s[f"hid{t}o"].at[chunk_of(i)] for i in range(XN)]
            made = busiest_only(t, down(t, hid)).astype(jnp.bfloat16)
            for i in range(XN):
                part = made[i * rows : (i + 1) * rows]
                if i == 0:
                    s["orecvo"][t, x] = part
                else:
                    s["oreto"][t, chunk_of(i)] = part
                    b_copy(st, i).start()
            return
        for q in (1, 0):
            as_copy(st, q).wait_recv()
            made = down(t, [piece("hid", st, q)]).astype(jnp.bfloat16)
            for i in (2 * q, 2 * q + 1):
                part = made[(i % 2) * rows : (i % 2 + 1) * rows]
                if i == 0:
                    s["orecv" + kind][t, x] = part
                else:
                    s["oret" + kind][t, chunk_of(i)] = part
                    b_copy(st, i).start()

    def rows_to_sources(st):
        t, kind = st
        for i in range(1, XN):
            b_copy(st, i).wait_recv()
        got = s["orecv" + kind][t].reshape(XN * KINDS[kind], 512)
        if kind == "n":
            moved = dot(s["c_nb"][...], got)
        else:
            moved = dot(s["c_ob"][0], got[:, :256]) + dot(s["c_ob"][1], got[:, 256:])
        s["wsend" + kind][t] = moved.astype(jnp.bfloat16).reshape(ZN, 16, WIDTH[kind])
        for d in W_ORDER:
            w_copy(st, d).start()

    begun = set()

    def combine(st):
        t, kind = st
        if t not in begun:
            for copy in choices(t):
                copy.wait_recv()
        route = s["rn_v"][t]
        ranks, _ = route_ranks(route)
        for d in W_ORDER:
            w_copy(st, d).wait_recv()
        got = s["wrecv" + kind]
        for half in range(2):
            parts = gate_parts(route, s["gn_v"][t], ranks, half)
            parts = parts[:, 0:32] if kind == "n" else parts[:, 32:64]
            for b in range(8):
                rows = jnp.concatenate([got[t, b], got[t, 8 + b]], axis=0)
                if kind == "n":
                    rows = rows[:, half * 256 : (half + 1) * 256]
                mixed = dot(parts, rows)
                mixed = mixed[0:16] + mixed[16:32] + mixed[32:48]
                at = pl.ds(b * 512 + half * 256, 256)
                if t in begun:
                    comb[t, :, at] = (mix[t, :, at] + mixed).astype(jnp.bfloat16)
                else:
                    mix[t, :, at] = mixed
        if t in begun:
            out_copy(t).start()
        begun.add(t)

    def late_stash(st):
        if st[0] == B:
            for i in range(1, XN):
                sv_copy(i).wait_recv()
                s["kept_o"][0] += s["sv_r"][i].astype(jnp.float32)
        spread_sum(st)

    first = [rows_to_x, rows_to_sibling, products]
    last = [back_to_x, rows_to_sources, combine]
    steps = {
        "n": first + [pass_on, activate, relay, units_to_sibling] + last,
        "o": first + [late_stash, activate, units_to_sibling, spread_units] + last,
    }
    turned = False
    for at in ORDER:
        st = STREAMS[at // 10]
        steps[st[1]][at % 10](st)
        if at % 10 == 0 and not turned:
            turn_weights()
            turned = True

    for copy in wx:
        copy.wait_send()
    for st in STREAMS:
        for d in range(1, ZN):
            z_copy(st, d).wait_send()
        for d in W_ORDER:
            w_copy(st, d).wait_send()
        for i in range(XN):
            c_copy(st, i).wait_send()
        for i in range(1, XN):
            x_copy(st, i).wait_send()
            b_copy(st, i).wait_send()
        for q in range(PIECES[st[1]]):
            as_copy(st, q).wait_send()
            ag_copy(st, q, 1).wait_send()
            ag_copy(st, q, 2).wait_send()
            if st[1] == "n":
                near_copy(st, q).wait_send()
                far_copy(st, q).wait_send()
                relay_copy(st, q).wait_send()
            else:
                ag_copy(st, q, 0).wait_send()
                for k in range(3):
                    rs_copy(st, q, k).wait_send()
    for i in range(1, XN):
        sv_copy(i).wait_send()
        for t in (B, F):
            for copy in (xr_copy, xg_copy, xa_copy):
                copy(t, i).wait_send()
    for t in (B, F):
        for copy in choices(t):
            copy.wait_send()
        out_copy(t).wait()


def on_device(x_f, r_f, g_f, x_b, r_b, g_b, gate_up, down, saved):
    in_hbm = pl.BlockSpec(memory_space=pltpu.HBM)
    out = jax.ShapeDtypeStruct((16, 4096), jnp.bfloat16)
    call = pl.pallas_call(
        kernel,
        out_shape=[out, out],
        in_specs=[in_hbm] * 9,
        out_specs=[in_hbm, in_hbm],
        scratch_shapes=list(buffers().values()),
        compiler_params=pltpu.CompilerParams(
            collective_id=0, has_side_effects=True, vmem_limit_bytes=60 * 1024 * 1024
        ),
        cost_estimate=pl.CostEstimate(flops=4 * 10**9, bytes_accessed=8 * 10**6, transcendentals=10**6),
    )
    next_input, prior_gradient = call(
        x_f[0], r_f[0].T, g_f[0].T, x_b[0], r_b[0].T, g_b[0].T,
        gate_up.reshape(2, 4, 2, 128, 512), down.reshape(4, 2, 128, 512), saved[0, 0],
    )
    return next_input[None], prior_gradient[None]


def solution(mesh):
    row = P("pipe", "expert", None)
    wide = P("pipe", "expert", None, None)
    return jax.shard_map(
        on_device,
        mesh=mesh,
        in_specs=(row,) * 6 + (wide,) * 3,
        out_specs=(row, row),
        check_vma=False,
    )
```

```python
import jax
import jax.numpy as jnp
from jax import lax
from jax.experimental import pallas as pl
from jax.experimental.pallas import tpu as pltpu
from jax.sharding import PartitionSpec as P

GROUP = 8
BASE = 4
OVER = 5
ZN = 16
XN = 4
LINE = 4
NORM = ZN * BASE
LATE = ZN * OVER
CHUNK = NORM + LATE
F, B = 0, 1
KINDS = {"n": NORM, "o": LATE}
WIDTH = {"n": 512, "o": 256}
STREAMS = ((B, "o"), (B, "n"), (F, "o"), (F, "n"))
Z_ORDER = (8, 7, 9, 6, 10, 5, 11, 4, 12, 3, 13, 2, 14, 1, 15)
W_ORDER = Z_ORDER + (0,)
ENTRY = (3, 0, 1, 2)
ORDER = (
    30, 0, 31, 10, 32, 20, 1, 2, 11, 33,
    21, 12, 22, 3, 34, 13, 4, 35, 23, 36,
    14, 5, 24, 37, 15, 6, 25, 7, 16, 38,
    17, 26, 27, 8, 18, 28, 19, 39, 9, 29,
)
PIECES = {"n": 2, "o": 1}
MESH = pl.DeviceIdType.MESH


def one_hot(target, width):
    col = lax.broadcasted_iota(jnp.int32, (target.shape[0], width), 1)
    return jnp.where(col == target, 1.0, 0.0).astype(jnp.bfloat16)


def fifth(v):
    return (v * 205) >> 10


def rows_of(count):
    return lax.broadcasted_iota(jnp.int32, (count, 1), 0)


def norm_out():
    r = rows_of(256)
    return one_hot(((r >> 2) & 15) * 16 + (r >> 6) * 4 + (r & 3), 256)


def norm_back():
    r = rows_of(256)
    return one_hot(((r >> 2) & 3) * 64 + (r >> 4) * 4 + (r & 3), 256)


def over_out(half):
    r = rows_of(80)
    g = fifth(r)
    return one_hot(g * 16 + half * 8 + r - 5 * g, 256)


def over_back(half):
    r = rows_of(256)
    j = r & 7
    want = jnp.where((((r >> 3) & 1) == half) & (j < OVER), (r >> 4) * 5 + j, -1)
    one = one_hot(want, 80)
    return jnp.concatenate([one] * XN, axis=1)


def stash_rows(x):
    r = rows_of(CHUNK)
    k = r - NORM
    is_norm = k < 0
    g = jnp.where(is_norm, r >> 2, fifth(k))
    slot = jnp.where(is_norm, r & 3, 4 + k - 5 * g)
    return one_hot(((g & 7) * 8 + x * 2 + (g >> 3)) * 9 + slot, XN * CHUNK)


def dot(a, b):
    return jnp.dot(a, b, preferred_element_type=jnp.float32)


def dot_t(a, b):
    return lax.dot_general(a, b, (((1,), (1,)), ((), ())), preferred_element_type=jnp.float32)


def sigmoid(v):
    return 1.0 / (1.0 + jnp.exp(-v))


def route_ranks(route):
    name = lax.broadcasted_iota(jnp.int32, (8, 16), 0)
    picks = [route[k : k + 1] for k in range(2)]
    hits = jnp.where(picks[0] == name, 1.0, 0.0) + jnp.where(picks[1] == name, 1.0, 0.0)
    row = lax.broadcasted_iota(jnp.int32, (16, 16), 0)
    col = lax.broadcasted_iota(jnp.int32, (16, 16), 1)
    earlier = jnp.where(row < col, 1.0, 0.0).astype(jnp.bfloat16)
    before = dot(hits.astype(jnp.bfloat16), earlier)
    ranks = [
        jnp.sum(jnp.where(pick == name, before, 0.0), axis=0, keepdims=True).astype(jnp.int32) for pick in picks
    ]
    return ranks, jnp.sum(hits, axis=1, keepdims=True)


def choice_match(route, ranks, rows, half=None):
    row = lax.broadcasted_iota(jnp.int32, (rows, 16), 0)
    is_norm = row < 32
    expert = ((row >> 2) & 3) * 2 + (row >> 4)
    slot = jnp.where(is_norm, row & 3, 4 + (row & 7))
    if half is not None:
        slot = jnp.where(is_norm | (((row >> 3) & 1) == half), slot, 99)
    return [
        (slot == ranks[k]) & ((expert == route[k : k + 1]) | jnp.logical_not(is_norm)) for k in range(2)
    ]


def gate_parts(route, gates, ranks, half):
    match = choice_match(route, ranks, 64, half)
    total = jnp.where(match[0], gates[0:1], 0.0) + jnp.where(match[1], gates[1:2], 0.0)
    total = jnp.concatenate([total, jnp.zeros((64, 16), jnp.float32)], axis=0)
    total = jnp.concatenate([total, jnp.zeros((128, 112), jnp.float32)], axis=1)
    total = jnp.transpose(total)[:16, :64]
    high = total.astype(jnp.bfloat16)
    rest = total - high.astype(jnp.float32)
    middle = rest.astype(jnp.bfloat16)
    low = (rest - middle.astype(jnp.float32)).astype(jnp.bfloat16)
    return jnp.concatenate([high, middle, low], axis=0)


def buffers():
    bf16, f32 = jnp.bfloat16, jnp.float32
    out = {
        "xin": pltpu.VMEM((2, 16, 4096), bf16),
        "r_v": pltpu.VMEM((2, 2, 16), jnp.int32),
        "rn_v": pltpu.VMEM((2, 2, 16), jnp.int32),
        "gn_v": pltpu.VMEM((2, 2, 16), f32),
        "wgu": pltpu.VMEM((2, 4, 2, 128, 512), bf16),
        "wd": pltpu.VMEM((4, 2, 128, 512), bf16),
        "wgu_s": pltpu.VMEM((2, 4, 128, 512), bf16),
        "wd_s": pltpu.VMEM((4, 128, 512), bf16),
        "up_f": pltpu.VMEM((2, 512, 4 * 256), bf16),
        "up_b": pltpu.VMEM((2, 512, 4 * 128), bf16),
        "saved": pltpu.VMEM((576, 256), bf16),
        "c_no": pltpu.VMEM((256, 256), bf16),
        "c_oo": pltpu.VMEM((2, 80, 256), bf16),
        "c_nb": pltpu.VMEM((256, 256), bf16),
        "c_ob": pltpu.VMEM((2, 256, XN * LATE), bf16),
        "kept_n": pltpu.VMEM((2, 2 * NORM, 256), f32),
        "kept_o": pltpu.VMEM((1, LATE, 256), f32),
        "sv_s": pltpu.VMEM((XN, LATE, 256), bf16),
        "sv_r": pltpu.VMEM((XN, LATE, 256), bf16),
        "mix": pltpu.VMEM((2, 16, 4096), f32),
        "comb": pltpu.VMEM((2, 16, 4096), bf16),
    }
    for kind, rows in KINDS.items():
        for name in ("zsend", "zrecv", "wsend", "wrecv"):
            out[name + kind] = pltpu.VMEM((2, ZN, 16, WIDTH[kind]), bf16)
        for name in ("xsend", "xrecv", "xsib", "oret", "orecv"):
            out[name + kind] = pltpu.VMEM((2, XN, rows, 512), bf16)
    for t in (F, B):
        units = 256 if t == F else 128
        parts = 1 if t == F else 2
        out[f"xr_own{t}"] = pltpu.VMEM((4, LATE, units), f32)
        out[f"xr_s{t}"] = pltpu.VMEM((XN, 4, LATE, units), bf16)
        out[f"xr_r{t}"] = pltpu.VMEM((XN, 4, LATE, units), bf16)
        for kind, rows in (("n", 2 * NORM), ("o", LATE)):
            out[f"own{t}{kind}"] = pltpu.VMEM((PIECES[kind], 2, rows, units), f32)
            for way in "sr":
                if kind == "o":
                    out[f"rs_{way}{t}o"] = pltpu.VMEM((1, 3, rows, units), bf16)
                else:
                    out[f"na_{way}{t}n"] = pltpu.VMEM((2, 2, rows, units), bf16)
                    out[f"fa_{way}{t}n"] = pltpu.VMEM((2, rows, units), bf16)
            count = 2 if kind == "n" else XN
            out[f"hid{t}{kind}"] = pltpu.VMEM((count, 2, parts, rows, 512), bf16)
    dma = pltpu.SemaphoreType.DMA
    out["load_sem"] = dma((7,))
    out["wx_sem"] = dma((2, 2))
    for kind in KINDS:
        for name in ("z", "w"):
            out[name + kind + "_sem"] = dma((2, 2, ZN))
        for name in ("x", "c", "b"):
            out[name + kind + "_sem"] = dma((2, 2, XN))
        out["as" + kind + "_sem"] = dma((2, 2, PIECES[kind]))
        for name in ("rs", "ag"):
            out[name + kind + "_sem"] = dma((2, 2, PIECES[kind], 3))
    for name in ("xr", "xg", "xa"):
        out[name + "_sem"] = dma((2, 2, XN))
    for name in ("na", "fa"):
        out[name + "_sem"] = dma((2, 2, 2))
    out["sv_sem"] = dma((2, XN))
    out["y_sem"] = dma((2, 2, 2))
    out["out_sem"] = dma((2,))
    return out


def kernel(x_f, r_f, g_f, x_b, r_b, g_b, wgu_h, wd_h, saved_h, out, *scratch):
    s = dict(zip(buffers(), scratch))
    xin, r_v = s["xin"], s["r_v"]
    wgu, wd, wgu_s, wd_s = s["wgu"], s["wd"], s["wgu_s"], s["wd_s"]
    comb, mix = s["comb"], s["mix"]

    pipe = lax.axis_index("pipe")
    expert = lax.axis_index("expert")
    y, h = pipe // 8, pipe % 8
    zl, core = h // 2, h % 2
    x, zh = expert // 2, expert % 2
    g = zh * 8 + h
    near, far = zl + 1 - 2 * (zl % 2), (zl + 2) % LINE
    cross = (near + 2) % LINE
    order = (cross, near, far, zl)

    def ring_id(gg, section=y):
        return (section * 8 + gg % 8, x * 2 + gg // 8)

    def x_id(xx):
        return (pipe, xx * 2 + zh)

    def line_id(zz):
        return (y * 8 + zz * 2 + core, expert)

    def chunk_of(i):
        return (x + XN - i) % XN

    sib_id = (pipe + 1 - 2 * core, expert)
    after = ((y + 1) % 8, (y + 7) % 8)

    def remote(src, dst, ss, rs, dev):
        return pltpu.make_async_remote_copy(
            src_ref=src, dst_ref=dst, send_sem=ss, recv_sem=rs, device_id=dev, device_id_type=MESH
        )

    def pair(name, *at):
        sem = s[name + "_sem"]
        return sem.at[(0,) + at], sem.at[(1,) + at]

    def piece(name, st, q):
        return s[f"{name}{st[0]}{st[1]}"].at[q]

    def block_at(zz):
        return pl.ds(pl.multiple_of(zz * 128, 128), 128)

    def z_copy(st, d):
        t, kind = st
        to = (g + d) % ZN
        return remote(s["zsend" + kind].at[t, to], s["zrecv" + kind].at[t, g], *pair("z" + kind, t, d), ring_id(to))

    def x_copy(st, d):
        t, kind = st
        to = (x + d) % XN
        return remote(s["xsend" + kind].at[t, to], s["xrecv" + kind].at[t, x], *pair("x" + kind, t, d), x_id(to))

    def c_copy(st, i):
        t, kind = st
        at = chunk_of(i)
        return remote(s["xrecv" + kind].at[t, at], s["xsib" + kind].at[t, at], *pair("c" + kind, t, i), sib_id)

    def units_of(st, q):
        return piece("hid", st, q if st[1] == "n" else x)

    def sv_copy(i):
        return remote(s["sv_s"].at[i], s["sv_r"].at[i], *pair("sv", i), x_id(chunk_of(i)))

    def xr_copy(t, i):
        return remote(s[f"xr_s{t}"].at[i], s[f"xr_r{t}"].at[i], *pair("xr", t, i), x_id(chunk_of(i)))

    def rs_copy(st, q, k):
        src, dst = piece("rs_s", st, q).at[k], piece("rs_r", st, q).at[k]
        return remote(src, dst, *pair("rs" + st[1], st[0], q, k), line_id(order[k]))

    def near_copy(st, q):
        src, dst = piece("na_s", st, q), piece("na_r", st, q)
        return remote(src, dst, *pair("na", st[0], q), line_id(near))

    def far_copy(st, q):
        src, dst = piece("fa_s", st, q), piece("fa_r", st, q)
        return remote(src, dst, *pair("fa", st[0], q), line_id(far))

    def ag_copy(st, q, k):
        here = units_of(st, q).at[core, :, :, block_at(zl)]
        return remote(here, here, *pair("ag" + st[1], st[0], q, k), line_id(order[k]))

    def relay_copy(st, q):
        here = units_of(st, q).at[core, :, :, block_at(far)]
        return remote(here, here, *pair("agn", st[0], q, 0), line_id(near))

    def as_copy(st, q):
        here = units_of(st, q).at[core]
        return remote(here, here, *pair("as" + st[1], st[0], q), sib_id)

    def xg_copy(t, i):
        here = s[f"hid{t}o"].at[x, core]
        return remote(here, here, *pair("xg", t, i), x_id((x + i) % XN))

    def xa_copy(t, i):
        here = s[f"hid{t}o"].at[chunk_of(i), core]
        return remote(here, here, *pair("xa", t, i), sib_id)

    def b_copy(st, i):
        t, kind = st
        to = chunk_of(i)
        return remote(s["oret" + kind].at[t, to], s["orecv" + kind].at[t, x], *pair("b" + kind, t, i), x_id(to))

    def w_copy(st, d):
        t, kind = st
        to = (g + d) % ZN
        src, dst = s["wsend" + kind].at[t, to], s["wrecv" + kind].at[t, g]
        return remote(src, dst, *pair("w" + kind, t, d), ring_id(to, after[t]))

    def choices(t):
        dev = ring_id(g, after[t])
        return [
            remote((r_f, r_b)[t], s["rn_v"].at[t], *pair("y", t, 0), dev),
            remote((g_f, g_b)[t], s["gn_v"].at[t], *pair("y", t, 1), dev),
        ]

    def out_copy(t):
        return pltpu.make_async_copy(comb.at[t], out.at[t], s["out_sem"].at[t])

    wx = [
        remote(wgu_h.at[:, :, 1 - core], wgu_s, *pair("wx", 0), sib_id),
        remote(wd_h.at[:, 1 - core], wd_s, *pair("wx", 1), sib_id),
    ]

    moves = (
        (r_b, r_v.at[B]), (x_b, xin.at[B]), (r_f, r_v.at[F]), (x_f, xin.at[F]),
        (saved_h, s["saved"]), (wgu_h, wgu), (wd_h, wd),
    )
    loads = [pltpu.make_async_copy(a, b, s["load_sem"].at[i]) for i, (a, b) in enumerate(moves)]
    for load in loads:
        load.start()

    barrier = pltpu.get_barrier_semaphore()
    peers = [ring_id((g + d) % ZN) for d in Z_ORDER]
    peers += [x_id((x + d) % XN) for d in range(1, XN)]
    peers += [ring_id(gg, section) for section in after for gg in range(ZN)]
    for peer in peers:
        pl.semaphore_signal(barrier, inc=1, device_id=peer, device_id_type=MESH)

    for load in loads[:4]:
        load.wait()
    routing = {}
    for t in (B, F):
        route = r_v[t]
        ranks, counts = route_ranks(route)
        match = choice_match(route, ranks, 48)
        pick = jnp.where(match[0] | match[1], 1.0, 0.0).astype(jnp.bfloat16)
        name = lax.broadcasted_iota(jnp.int32, (8, 1), 0)
        mine = jnp.sum(jnp.where(name == expert, counts, 0.0), axis=0, keepdims=True)
        routing[t] = mine > BASE + 0.5
        upper = lax.broadcasted_iota(jnp.int32, (16, 256), 0) < 8
        for b in range(8):
            rows = dot(pick, xin[t, :, b * 512 : (b + 1) * 512])
            over = jnp.where(upper, rows[32:48, :256], rows[32:48, 256:]).astype(jnp.bfloat16)
            for hi in range(2):
                s["zsendn"][t, hi * 8 + b] = rows[hi * 16 : hi * 16 + 16].astype(jnp.bfloat16)
                s["zsendo"][t, hi * 8 + b] = over

    def busiest_only(t, value):
        return jnp.where(routing[t], value, 0.0)

    pl.semaphore_wait(barrier, len(peers))

    def rows_to_ring(st):
        t, kind = st
        for d in Z_ORDER:
            z_copy(st, d).start()
        s["zrecv" + kind][t, g] = s["zsend" + kind][t, g]

    rows_to_ring(STREAMS[ENTRY[0]])
    for copy in wx:
        copy.start()
    rows_to_ring(STREAMS[ENTRY[1]])
    for t in (B, F):
        for copy in choices(t):
            copy.start()

    s["c_no"][...] = norm_out()
    s["c_nb"][...] = norm_back()
    for half in range(2):
        s["c_oo"][half] = over_out(half)
        s["c_ob"][half] = over_back(half)
    loads[4].wait()
    for i in range(XN):
        found = dot(stash_rows(chunk_of(i)), s["saved"][...])
        s["kept_n"][i // 2, (i % 2) * NORM : (i % 2 + 1) * NORM] = found[:NORM]
        late = busiest_only(B, found[NORM:])
        if i == 0:
            s["kept_o"][0] = late
        else:
            s["sv_s"][i] = late.astype(jnp.bfloat16)
            sv_copy(i).start()

    def rows_to_x(st):
        t, kind = st
        for d in range(1, ZN):
            z_copy(st, d).wait_recv()
        got = s["zrecv" + kind][t].reshape(256, WIDTH[kind])
        if kind == "n":
            moved = dot(s["c_no"][...], got).astype(jnp.bfloat16)
        else:
            moved = jnp.concatenate([dot(s["c_oo"][0], got), dot(s["c_oo"][1], got)], axis=1).astype(jnp.bfloat16)
        for xx in range(XN):
            s["xsend" + kind][t, xx] = moved[xx * NORM : (xx + 1) * NORM] if kind == "n" else moved
        for d in (2, 1, 3):
            x_copy(st, d).start()
        s["xrecv" + kind][t, x] = s["xsend" + kind][t, x]
        c_copy(st, 0).start()

    def rows_to_sibling(st):
        for i in (1, 3, 2):
            x_copy(st, i).wait_recv()
            c_copy(st, i).start()

    rows_to_ring(STREAMS[ENTRY[2]])
    rows_to_ring(STREAMS[ENTRY[3]])

    def turn_weights():
        for load in loads[5:]:
            load.wait()
        for copy in wx:
            copy.wait_recv()
        for k, dest in enumerate(order):
            at = k * 128
            s["up_b"][0, :, at : at + 128] = jnp.transpose(wd[dest, core])
            s["up_b"][1, :, at : at + 128] = jnp.transpose(wd_s[dest])
            for a in range(2):
                at = k * 256 + a * 128
                s["up_f"][0, :, at : at + 128] = jnp.transpose(wgu[a, dest, core])
                s["up_f"][1, :, at : at + 128] = jnp.transpose(wgu_s[a, dest])

    def products(st):
        t, kind = st
        up = s["up_f"] if t == F else s["up_b"]
        units = 256 if t == F else 128
        for i in range(XN):
            c_copy(st, i).wait_recv()
        ats = [chunk_of(i) for i in range(XN)]
        mine = jnp.concatenate([s["xrecv" + kind][t, at] for at in ats], axis=0)
        other = jnp.concatenate([s["xsib" + kind][t, at] for at in ats], axis=0)
        for k in range(4):
            lanes = slice(k * units, (k + 1) * units)
            part = dot(mine, up[0, :, lanes]) + dot(other, up[1, :, lanes])
            if kind == "o":
                part = busiest_only(t, part)
                s[f"xr_own{t}"][k] = part[:LATE]
                for i in range(1, XN):
                    s[f"xr_s{t}"][i, k] = part[i * LATE : (i + 1) * LATE].astype(jnp.bfloat16)
                continue
            for q in range(2):
                rows = part[q * 2 * NORM : (q + 1) * 2 * NORM]
                if k < 2:
                    piece("na_s", st, q)[k] = rows.astype(jnp.bfloat16)
                    if k == 1:
                        near_copy(st, q).start()
                else:
                    piece("own", st, q)[k - 2] = rows
        if kind == "o":
            for i in (2, 1, 3):
                xr_copy(t, i).start()

    def spread_sum(st):
        t = st[0]
        for i in range(1, XN):
            xr_copy(t, i).wait_recv()
        for k in range(4):
            total = s[f"xr_own{t}"][k]
            for i in range(1, XN):
                total = total + s[f"xr_r{t}"][i, k].astype(jnp.float32)
            if k == 3:
                piece("own", st, 0)[1] = total
            else:
                piece("rs_s", st, 0)[k] = total.astype(jnp.bfloat16)
                rs_copy(st, 0, k).start()

    def pass_on(st):
        for q in range(2):
            near_copy(st, q).wait_recv()
            total = piece("own", st, q)[0] + piece("na_r", st, q)[0].astype(jnp.float32)
            piece("fa_s", st, q)[...] = total.astype(jnp.bfloat16)
            far_copy(st, q).start()

    def activate(st):
        for q in range(PIECES[st[1]]):
            total = piece("own", st, q)[1]
            if st[1] == "n":
                far_copy(st, q).wait_recv()
                total = total + piece("na_r", st, q)[1].astype(jnp.float32)
                total = total + piece("fa_r", st, q)[...].astype(jnp.float32)
            else:
                for k in range(3):
                    rs_copy(st, q, k).wait_recv()
                    total = total + piece("rs_r", st, q)[k].astype(jnp.float32)
            hid = units_of(st, q)
            if st[0] == F:
                gate, up = total[:, :128], total[:, 128:]
                hid[core, 0, :, block_at(zl)] = (gate * sigmoid(gate) * up).astype(jnp.bfloat16)
            else:
                stash = s["kept_" + st[1]][q]
                gate, up = stash[:, :128], stash[:, 128:]
                sig = sigmoid(gate)
                slope = sig * (1.0 + gate * (1.0 - sig))
                hid[core, 0, :, block_at(zl)] = (total * up * slope).astype(jnp.bfloat16)
                hid[core, 1, :, block_at(zl)] = (total * (gate * sig)).astype(jnp.bfloat16)
            for k in (2, 1) if st[1] == "n" else (2, 1, 0):
                ag_copy(st, q, k).start()

    def relay(st):
        for q in range(2):
            ag_copy(st, q, 2).wait_recv()
            relay_copy(st, q).start()

    def units_to_sibling(st):
        for q in range(PIECES[st[1]]):
            ag_copy(st, q, 1).wait_recv()
            if st[1] == "n":
                relay_copy(st, q).wait_recv()
            else:
                ag_copy(st, q, 2).wait_recv()
                ag_copy(st, q, 0).wait_recv()
            as_copy(st, q).start()
        if st[1] == "o":
            for i in (2, 1, 3):
                xg_copy(st[0], i).start()

    def spread_units(st):
        for i in (1, 3, 2):
            xg_copy(st[0], i).wait_recv()
            xa_copy(st[0], i).start()

    def down(t, hid):
        def rows(c, a):
            return jnp.concatenate([one[c, a] for one in hid], axis=0)

        if t == F:
            return dot(rows(0, 0), wd[:, 0].reshape(512, 512)) + dot(rows(1, 0), wd[:, 1].reshape(512, 512))
        total = None
        for c in range(2):
            for a in range(2):
                part = dot(rows(c, a), wgu[a, :, c].reshape(512, 512))
                total = part if total is None else total + part
        return total

    def back_to_x(st):
        t, kind = st
        rows = KINDS[kind]
        if kind == "o":
            as_copy(st, 0).wait_recv()
            for i in range(1, XN):
                xa_copy(t, i).wait_recv()
            hid = [s[f"hid{t}o"].at[chunk_of(i)] for i in range(XN)]
            made = busiest_only(t, down(t, hid)).astype(jnp.bfloat16)
            for i in range(XN):
                part = made[i * rows : (i + 1) * rows]
                if i == 0:
                    s["orecvo"][t, x] = part
                else:
                    s["oreto"][t, chunk_of(i)] = part
                    b_copy(st, i).start()
            return
        for q in (1, 0):
            as_copy(st, q).wait_recv()
            made = down(t, [piece("hid", st, q)]).astype(jnp.bfloat16)
            for i in (2 * q, 2 * q + 1):
                part = made[(i % 2) * rows : (i % 2 + 1) * rows]
                if i == 0:
                    s["orecv" + kind][t, x] = part
                else:
                    s["oret" + kind][t, chunk_of(i)] = part
                    b_copy(st, i).start()

    def rows_to_sources(st):
        t, kind = st
        for i in range(1, XN):
            b_copy(st, i).wait_recv()
        got = s["orecv" + kind][t].reshape(XN * KINDS[kind], 512)
        if kind == "n":
            moved = dot(s["c_nb"][...], got)
        else:
            moved = dot(s["c_ob"][0], got[:, :256]) + dot(s["c_ob"][1], got[:, 256:])
        s["wsend" + kind][t] = moved.astype(jnp.bfloat16).reshape(ZN, 16, WIDTH[kind])
        for d in W_ORDER:
            w_copy(st, d).start()

    begun = set()

    def combine(st):
        t, kind = st
        if t not in begun:
            for copy in choices(t):
                copy.wait_recv()
        route = s["rn_v"][t]
        ranks, _ = route_ranks(route)
        for d in W_ORDER:
            w_copy(st, d).wait_recv()
        got = s["wrecv" + kind]
        for half in range(2):
            parts = gate_parts(route, s["gn_v"][t], ranks, half)
            parts = parts[:, 0:32] if kind == "n" else parts[:, 32:64]
            for b in range(8):
                rows = jnp.concatenate([got[t, b], got[t, 8 + b]], axis=0)
                if kind == "n":
                    rows = rows[:, half * 256 : (half + 1) * 256]
                mixed = dot(parts, rows)
                mixed = mixed[0:16] + mixed[16:32] + mixed[32:48]
                at = pl.ds(b * 512 + half * 256, 256)
                if t in begun:
                    comb[t, :, at] = (mix[t, :, at] + mixed).astype(jnp.bfloat16)
                else:
                    mix[t, :, at] = mixed
        if t in begun:
            out_copy(t).start()
        begun.add(t)

    def late_stash(st):
        if st[0] == B:
            for i in range(1, XN):
                sv_copy(i).wait_recv()
                s["kept_o"][0] += s["sv_r"][i].astype(jnp.float32)
        spread_sum(st)

    first = [rows_to_x, rows_to_sibling, products]
    last = [back_to_x, rows_to_sources, combine]
    steps = {
        "n": first + [pass_on, activate, relay, units_to_sibling] + last,
        "o": first + [late_stash, activate, units_to_sibling, spread_units] + last,
    }
    turned = False
    for at in ORDER:
        st = STREAMS[at // 10]
        steps[st[1]][at % 10](st)
        if at % 10 == 0 and not turned:
            turn_weights()
            turned = True

    for copy in wx:
        copy.wait_send()
    for st in STREAMS:
        for d in range(1, ZN):
            z_copy(st, d).wait_send()
        for d in W_ORDER:
            w_copy(st, d).wait_send()
        for i in range(XN):
            c_copy(st, i).wait_send()
        for i in range(1, XN):
            x_copy(st, i).wait_send()
            b_copy(st, i).wait_send()
        for q in range(PIECES[st[1]]):
            as_copy(st, q).wait_send()
            ag_copy(st, q, 1).wait_send()
            ag_copy(st, q, 2).wait_send()
            if st[1] == "n":
                near_copy(st, q).wait_send()
                far_copy(st, q).wait_send()
                relay_copy(st, q).wait_send()
            else:
                ag_copy(st, q, 0).wait_send()
                for k in range(3):
                    rs_copy(st, q, k).wait_send()
    for i in range(1, XN):
        sv_copy(i).wait_send()
        for t in (B, F):
            for copy in (xr_copy, xg_copy, xa_copy):
                copy(t, i).wait_send()
    for t in (B, F):
        for copy in choices(t):
            copy.wait_send()
        out_copy(t).wait()


def on_device(x_f, r_f, g_f, x_b, r_b, g_b, gate_up, down, saved):
    in_hbm = pl.BlockSpec(memory_space=pltpu.HBM)
    call = pl.pallas_call(
        kernel,
        out_shape=jax.ShapeDtypeStruct((2, 16, 4096), jnp.bfloat16),
        in_specs=[in_hbm] * 9,
        out_specs=in_hbm,
        scratch_shapes=list(buffers().values()),
        compiler_params=pltpu.CompilerParams(
            collective_id=0, has_side_effects=True, vmem_limit_bytes=60 * 1024 * 1024
        ),
        cost_estimate=pl.CostEstimate(flops=4 * 10**9, bytes_accessed=8 * 10**6, transcendentals=10**6),
    )
    both = call(
        x_f[0], r_f[0].T, g_f[0].T, x_b[0], r_b[0].T, g_b[0].T,
        gate_up.reshape(2, 4, 2, 128, 512), down.reshape(4, 2, 128, 512), saved[0, 0],
    )
    return both[F : F + 1], both[B : B + 1]


def solution(mesh):
    row = P("pipe", "expert", None)
    wide = P("pipe", "expert", None, None)
    return jax.shard_map(
        on_device,
        mesh=mesh,
        in_specs=(row,) * 6 + (wide,) * 3,
        out_specs=(row, row),
        check_vma=False,
    )
```
